32 devices in a mesh: sweep: 8 (over y, x, core), span: 4 (over z).
Axes of the slice: x: 2, y: 2, z: 4, core: 2. Of those that a mesh axis runs over, the one named last changes fastest.
Arguments:
- right_side: float32 [16, 4, 625, 512], P('sweep', 'span'), may hold values from -6 to 6
- start_field: float32 [16, 4, 625, 512], P('sweep', 'span'), may hold values from -6 to 6
- block_inverse: float32 [16, 4, 625, 625], P('sweep', 'span'), may hold values from -0.25 to 0.25
- upwind_block: float32 [16, 4, 625, 125], P('sweep', 'span'), may hold values from -1 to 1
- south_block: float32 [16, 4, 625, 125], P('sweep', 'span'), may hold values from -0.625 to 0.625
- north_block: float32 [16, 4, 625, 125], P('sweep', 'span'), may hold values from -0.625 to 0.625
Outputs:
- solution: float32 [16, 4, 625, 512], P('sweep', 'span')
The draws below stay inside these ranges and needn't reach their ends.
All inputs are finite; a program needn't handle non-finite values.
Results may differ from the reference program's by a relative error of at most 0.00022.
Values sent between devices are 32-bit elements; how exact they have to be, the bound alone decides.
No kernel may reach another device: no remote copies, remote signals or barrier semaphores. Data moves between devices by JAX's collectives and lax.ppermute only.
A program may use at most 128 MiB of HBM per device.

```python
import jax
import jax.numpy as jnp
from jax import lax

VARS = 5
NODE = 5
UNK = 625
FACE = 125
SWEEPS = 2
R = 512
NI = 16
NJ = 4


def block_levels(key, shape, shards, low, top_value):
    gain = 1.0
    for dim, blocks in shards:
        draws = jax.random.uniform(jax.random.fold_in(jax.random.fold_in(key, 6), dim), (blocks,), jnp.float32, low / len(shards), top_value / len(shards))
        gain = gain * jnp.repeat(jnp.exp(draws), shape[dim] // blocks).reshape((-1,) + (1,) * (len(shape) - 1 - dim))
    return gain


def normal_values(stream_key, dims, scale, most, split=(), held_as=jnp.bfloat16):
    gain = block_levels(stream_key, dims, split, -0.22, 0.18) if split else 1.0
    result = jax.random.normal(stream_key, dims, jnp.float32) * scale * gain
    return jnp.minimum(jnp.maximum(result, -most), most).astype(held_as)


def setup_inputs(seed: int = 0) -> dict:
    keys = jax.random.split(jax.random.key(seed), 7)
    right_side = normal_values(keys[0], (NI, NJ, UNK, R), 1.0, 6.0, ((0, 8), (1, 4)), jnp.float32)
    start_field = normal_values(keys[1], (NI, NJ, UNK, R), 1.0, 6.0, ((0, 8), (1, 4)), jnp.float32)
    block_inverse = normal_values(keys[2], (NI, NJ, UNK, UNK), UNK ** -0.5, 0.25, ((0, 8), (1, 4)), jnp.float32)
    upwind_block = normal_values(keys[3], (NI, NJ, UNK, FACE), (0.85 / FACE ** 0.5), 1.0, ((0, 8), (1, 4)), jnp.float32)
    south_block = normal_values(keys[4], (NI, NJ, UNK, FACE), (0.5 / FACE ** 0.5), 0.625, ((0, 8), (1, 4)), jnp.float32)
    north_block = normal_values(keys[5], (NI, NJ, UNK, FACE), (0.5 / FACE ** 0.5), 0.625, ((0, 8), (1, 4)), jnp.float32)
    return dict(right_side=right_side, start_field=start_field, block_inverse=block_inverse, upwind_block=upwind_block, south_block=south_block, north_block=north_block)


def face_grid(field):
    leading = field.shape[:-2]
    return field.reshape(leading + (VARS, NODE, NODE, NODE, field.shape[-1]))


def down_face(field):
    leading = field.shape[:-2]
    return face_grid(field)[..., :, NODE - 1, :, :, :].reshape(leading + (FACE, field.shape[-1]))


def high_face(field):
    leading = field.shape[:-2]
    return face_grid(field)[..., :, :, NODE - 1, :, :].reshape(leading + (FACE, field.shape[-1]))


def low_face(field):
    leading = field.shape[:-2]
    return face_grid(field)[..., :, :, 0, :, :].reshape(leading + (FACE, field.shape[-1]))


def batched_product(matrix, vectors):
    return jnp.einsum("...ab,...br->...ar", matrix, vectors, precision=lax.Precision.HIGHEST)


def reference(right_side, start_field, block_inverse, upwind_block, south_block, north_block):
    field = start_field
    span_count = start_field.shape[1]
    columns = start_field.shape[-1]
    for sweep_no in range(SWEEPS):
        south_traces = jnp.roll(high_face(field), 1, axis=1)
        north_traces = jnp.roll(low_face(field), -1, axis=1)
        forcing = right_side - batched_product(south_block, south_traces) - batched_product(north_block, north_traces)

        def element_row(inflow, row_data):
            forcing_row, inverse_row, upwind_row = row_data
            residual = forcing_row - batched_product(upwind_row, inflow)
            solved = batched_product(inverse_row, residual)
            return down_face(solved), solved

        start_trace = jnp.zeros((span_count, FACE, columns), jnp.float32)
        _, field = lax.scan(element_row, start_trace, (forcing, block_inverse, upwind_block))
    return field
```

```python
import functools

import jax
import jax.numpy as jnp
from jax import lax
from jax.experimental import pallas as pl
from jax.experimental.pallas import tpu as pltpu
from jax.sharding import PartitionSpec as P

VARS = 5
NODE = 5
SWEEPS = 2
CORES = 2
LIMIT = 32 * 1024 * 1024


def face_runs(kind):
    if kind == "down":
        return [
            (var * NODE**3 + (NODE - 1) * NODE**2, NODE**2) for var in range(VARS)
        ]
    b = NODE - 1 if kind == "high" else 0
    return [
        (var * NODE**3 + a * NODE**2 + b * NODE, NODE)
        for var in range(VARS)
        for a in range(NODE)
    ]


def face_size():
    return VARS * NODE**2


def padded(size):
    return -(-size // 128) * 128


def take_face(kind, read, write):
    at = 0
    for first, length in face_runs(kind):
        write(at, length, read(first, length))
        at += length


def split(x):
    top = x.astype(jnp.bfloat16)
    return top, (x - top.astype(jnp.float32)).astype(jnp.bfloat16)


def mul(a, b):
    ah, al = a if isinstance(a, tuple) else split(a)
    bh, bl = b if isinstance(b, tuple) else split(b)
    dot = functools.partial(jnp.dot, preferred_element_type=jnp.float32)
    return dot(ah, bh) + (dot(ah, bl) + dot(al, bh))


def call(kernel, outs, *args, scratch=(), smem=0, name=None):
    return pl.pallas_call(
        kernel,
        out_shape=[jax.ShapeDtypeStruct(s, jnp.float32) for s in outs],
        in_specs=[pl.BlockSpec(memory_space=pltpu.SMEM)] * smem
        + [pl.BlockSpec(memory_space=pltpu.VMEM)] * (len(args) - smem),
        out_specs=[pl.BlockSpec(memory_space=pltpu.VMEM)] * len(outs),
        scratch_shapes=list(scratch),
        compiler_params=pltpu.CompilerParams(vmem_limit_bytes=LIMIT),
        name=name,
    )(*args)


def start_faces(field_ref, high_ref, low_ref):
    face = face_size()
    for e in range(field_ref.shape[0]):
        for kind, out in (("high", high_ref), ("low", low_ref)):
            out[e, face:, :] = jnp.zeros((out.shape[1] - face, out.shape[2]), jnp.float32)
            at = 0
            for first, length in face_runs(kind):
                out[e, at : at + length, :] = field_ref[e, first : first + length, :]
                at += length


def fold_blocks(inv_ref, rhs_ref, up_ref, south_ref, north_ref,
                c_ref, b_ref, fc_ref, fb_ref, resp_ref, step_ref):
    face = face_size()
    wide = padded(face)
    elements = inv_ref.shape[0]
    for e in range(elements):
        inverse = split(inv_ref[e])
        c_ref[e] = mul(inverse, rhs_ref[e])
        b_ref[e] = jnp.zeros(b_ref.shape[1:], jnp.float32)
        for k, block in enumerate((south_ref, north_ref, up_ref)):
            b_ref[e, :, k * wide : k * wide + face] = mul(inverse, block[e])
        fc_ref[e] = jnp.zeros(fc_ref.shape[1:], jnp.float32)
        fb_ref[e] = jnp.zeros(fb_ref.shape[1:], jnp.float32)
        for f, kind in enumerate(("down", "high", "low")):
            at = f * wide
            for first, length in face_runs(kind):
                fc_ref[e, at : at + length, :] = c_ref[e, first : first + length, :]
                fb_ref[e, at : at + length, :] = b_ref[e, first : first + length, :]
                at += length
        own = fb_ref[e, :, 2 * wide :]
        if e == 0:
            resp_ref[e] = -own
        else:
            resp_ref[e] = -mul(own, resp_ref[e - 1, :wide, :])
    step_ref[...] = resp_ref[elements - 1, :wide, :]


def faces_without_inflow(rows, fc_ref, fb_ref, s_ref, n_ref, q_ref, g_ref):
    wide = s_ref.shape[1]
    elements = fc_ref.shape[0]
    for e in range(elements):
        q = fc_ref[e, :rows, :] - (
            mul(fb_ref[e, :rows, :wide], s_ref[e])
            + mul(fb_ref[e, :rows, wide : 2 * wide], n_ref[e])
        )
        if e:
            q = q - mul(fb_ref[e, :rows, 2 * wide :], q_ref[e - 1, :wide, :])
        q_ref[e] = q
    g_ref[...] = q_ref[elements - 1, :wide, :]


def pair_trace(core_ref, own_ref, other_ref, steps_ref, first_ref, chip_ref):
    half = other_ref.shape[1]
    chip = core_ref[1]

    @pl.when(core_ref[0] == 0)
    def _():
        first_ref[...] = own_ref[:, :half]
        chip_ref[...] = other_ref[...]

    @pl.when(core_ref[0] == 1)
    def _():
        first_ref[...] = other_ref[...]
        chip_ref[...] = own_ref[:, half:]

    chip_ref[...] += mul(steps_ref[2 * chip + 1], first_ref[...])


def inflow_of_cores(core_ref, first_ref, chips_ref, steps_ref, keep_ref, send_ref):
    chip = core_ref[1]
    keep_ref[...] = jnp.zeros_like(keep_ref)
    for m in range(chips_ref.shape[0] - 1):

        @pl.when(m < chip)
        def _():
            passed = mul(steps_ref[2 * m], keep_ref[...])
            keep_ref[...] = chips_ref[m] + mul(steps_ref[2 * m + 1], passed)

    send_ref[...] = first_ref[...] + mul(steps_ref[2 * chip], keep_ref[...])

    @pl.when(core_ref[0] == 1)
    def _():
        held = keep_ref[...]
        keep_ref[...] = send_ref[...]
        send_ref[...] = held


def join(core_ref, keep_ref, got_ref, inflow_ref):
    half = keep_ref.shape[1]

    @pl.when(core_ref[0] == 0)
    def _():
        inflow_ref[:, :half] = keep_ref[...]
        inflow_ref[:, half:] = got_ref[...]

    @pl.when(core_ref[0] == 1)
    def _():
        inflow_ref[:, :half] = got_ref[...]
        inflow_ref[:, half:] = keep_ref[...]


def next_faces(core_ref, q_ref, resp_ref, keep_ref, got_ref, high_ref, low_ref, inflow_ref):
    join(core_ref, keep_ref, got_ref, inflow_ref)
    wide = inflow_ref.shape[0]
    inflow = split(inflow_ref[...])
    for e in range(q_ref.shape[0]):
        high_ref[e] = q_ref[e, wide : 2 * wide, :] + mul(resp_ref[e, wide : 2 * wide, :], inflow)
        low_ref[e] = q_ref[e, 2 * wide :, :] + mul(resp_ref[e, 2 * wide :, :], inflow)


def whole_field(core_ref, c_ref, b_ref, s_ref, n_ref, keep_ref, got_ref, out_ref, inflow_ref):
    join(core_ref, keep_ref, got_ref, inflow_ref)
    wide = inflow_ref.shape[0]
    for e in range(c_ref.shape[0]):
        if e:
            at = 0
            for first, length in face_runs("down"):
                inflow_ref[at : at + length, :] = out_ref[e - 1, first : first + length, :]
                at += length
        out_ref[e] = c_ref[e] - (
            mul(b_ref[e, :, :wide], s_ref[e])
            + mul(b_ref[e, :, wide : 2 * wide], n_ref[e])
            + mul(b_ref[e, :, 2 * wide :], inflow_ref[...])
        )


def ring(axis, by):
    count = lax.axis_size(axis)
    return [(i, (i + by) % count) for i in range(count)]


def per_device(right_side, start_field, block_inverse, upwind_block, south_block, north_block):
    rhs, start = right_side[:, 0], start_field[:, 0]
    inverse, upwind = block_inverse[:, 0], upwind_block[:, 0]
    south, north = south_block[:, 0], north_block[:, 0]
    elements, unknowns, columns = rhs.shape
    wide = padded(face_size())
    half = columns // CORES
    devices = lax.axis_size("sweep")
    place = lax.axis_index("sweep")
    where = jnp.stack([place % CORES, place // CORES]).astype(jnp.int32)
    swap = [(i, i ^ 1) for i in range(devices)]
    like = [[c + CORES * k for k in range(devices // CORES)] for c in range(CORES)]
    trace = (elements, wide, columns)

    high, low = call(start_faces, [trace, trace], start, name="start_faces")
    for sweep_no in range(SWEEPS):
        last = sweep_no == SWEEPS - 1
        below = lax.ppermute(high, "span", ring("span", 1))
        above = lax.ppermute(low, "span", ring("span", -1))
        if sweep_no == 0:
            c, b, fc, fb, resp, step = call(
                fold_blocks,
                [
                    (elements, unknowns, columns),
                    (elements, unknowns, 3 * wide),
                    (elements, 3 * wide, columns),
                    (elements, 3 * wide, 3 * wide),
                    (elements, 3 * wide, wide),
                    (wide, wide),
                ],
                inverse, rhs, upwind, south, north,
                name="fold_blocks",
            )
            steps = lax.all_gather(step, "sweep")
        rows = wide if last else 3 * wide
        q, g = call(
            functools.partial(faces_without_inflow, rows),
            [(elements, rows, columns), (wide, columns)],
            fc, fb, below, above,
            name="faces_without_inflow",
        )
        away = lax.dynamic_slice_in_dim(g, (1 - place % CORES) * half, half, 1)
        other = lax.ppermute(away, "sweep", swap)
        first, chip = call(
            pair_trace, [(wide, half)] * 2, where, g, other, steps, smem=1, name="pair_trace"
        )
        chips = lax.all_gather(chip, "sweep", axis_index_groups=like)
        keep, send = call(
            inflow_of_cores, [(wide, half)] * 2, where, first, chips, steps, smem=1,
            name="inflow_of_cores",
        )
        got = lax.ppermute(send, "sweep", swap)
        held = [pltpu.VMEM((wide, columns), jnp.float32)]
        if not last:
            high, low = call(
                next_faces, [trace, trace], where, q, resp, keep, got,
                smem=1, scratch=held, name="next_faces",
            )
        else:
            (field,) = call(
                whole_field, [(elements, unknowns, columns)],
                where, c, b, below, above, keep, got,
                smem=1, scratch=held, name="whole_field",
            )
    return field[:, None]


def solution(mesh):
    spec = P("sweep", "span", None, None)
    return jax.shard_map(
        per_device, mesh=mesh, in_specs=(spec,) * 6, out_specs=spec, check_vma=False
    )
```

```python
import functools

import jax
import jax.numpy as jnp
from jax import lax
from jax.experimental import pallas as pl
from jax.experimental.pallas import tpu as pltpu
from jax.sharding import PartitionSpec as P

VARS = 5
NODE = 5
FACE = VARS * NODE**2
WIDE = 128
SWEEPS = 2
CORES = 2
LIMIT = 24 * 1024 * 1024
MOST = 48 * 1024 * 1024
ANY = pl.ANY
HBM = pltpu.HBM
VMEM = pltpu.VMEM
SMEM = pltpu.SMEM


def face_runs(kind):
    if kind == "down":
        return [(var * NODE**3 + (NODE - 1) * NODE**2, NODE**2) for var in range(VARS)]
    b = NODE - 1 if kind == "high" else 0
    return [
        (var * NODE**3 + a * NODE**2 + b * NODE, NODE)
        for var in range(VARS)
        for a in range(NODE)
    ]


def split(x):
    top = x.astype(jnp.bfloat16)
    return top, (x - top.astype(jnp.float32)).astype(jnp.bfloat16)


def left(x):
    high, low = split(x)
    return jnp.concatenate([high, high, low], axis=1)


def right(x):
    high, low = split(x)
    return jnp.concatenate([high, low, high], axis=0)


def stacked(a, b):
    return jnp.dot(a, b, preferred_element_type=jnp.float32)


def padded(x, rows):
    short = rows - x.shape[0]
    return jnp.concatenate([x, jnp.zeros((short, x.shape[1]), x.dtype)], axis=0) if short else x


def call(kernel, outs, *args, scratch=(), us=1, after=(), limit=LIMIT):
    args = list(args) + [(ANY, x) for x in after]

    def body(*refs):
        given = len(args) - len(after)
        kernel(*refs[:given], *refs[len(args) :])

    return pl.pallas_call(
        body,
        out_shape=[jax.ShapeDtypeStruct(shape, kind) for _, shape, kind in outs],
        in_specs=[pl.BlockSpec(memory_space=space) for space, _ in args],
        out_specs=[pl.BlockSpec(memory_space=space) for space, _, _ in outs],
        scratch_shapes=list(scratch),
        compiler_params=pltpu.CompilerParams(vmem_limit_bytes=limit),
        cost_estimate=pl.CostEstimate(flops=int(us * 10**9), bytes_accessed=0, transcendentals=0),
        name=getattr(kernel, "func", kernel).__name__,
    )(*[array for _, array in args])


def start_faces(core_ref, field_ref, *refs):
    outs, sems = refs[:-1], refs[-1]
    half = outs[0].shape[-1]
    copies = []
    for k, out in enumerate(outs):
        other, low = divmod(k, 2)
        first = 0 if low else (NODE - 1) * NODE
        own = core_ref[0] if other == 0 else 1 - core_ref[0]
        at = pl.multiple_of(own * half, half)
        copies.append(
            pltpu.make_async_copy(
                field_ref.at[:, :, pl.ds(first, NODE), :, pl.ds(at, half)], out, sems.at[k]
            )
        )
    for copy in copies:
        copy.start()
    for copy in copies:
        copy.wait()


def load_rows(pairs, sems):
    copies = []
    for k, (source, held) in enumerate(pairs):
        copies.append(pltpu.make_async_copy(source, held, sems.at[k]))
        copies[-1].start()
    return copies


def load_blocks(inv_ref, rhs_ref, up_ref, south_ref, north_ref, inv, rhs, blocks, sems):
    return [
        load_rows(
            [
                (inv_ref.at[e, :, 0, :], inv.at[e]),
                (rhs_ref.at[e, :, 0, :], rhs.at[e]),
                (south_ref.at[e, :, 0, :], blocks.at[e, 0]),
                (north_ref.at[e, :, 0, :], blocks.at[e, 1]),
                (up_ref.at[e, :, 0, :], blocks.at[e, 2]),
            ],
            sems.at[e],
        )
        for e in range(inv_ref.shape[0])
    ]


def fill_columns(e, depth, rhs, blocks, columns):
    wide = rhs.shape[2]
    columns[:, :wide] = right(padded(rhs[e], depth))
    for k in range(3):
        at = wide + k * WIDE
        block = right(padded(blocks[e, k], depth))
        columns[:, at : at + FACE] = block


def fold_blocks(inv_ref, rhs_ref, up_ref, south_ref, north_ref,
                c_ref, bsn_ref, bu_ref, faces_ref,
                inv, rhs, blocks, rows, columns, whole, sems):
    elements, unknowns = inv.shape[:2]
    depth, wide = rows.shape[1], rhs.shape[2]
    half = wide // CORES
    copies = load_blocks(inv_ref, rhs_ref, up_ref, south_ref, north_ref, inv, rhs, blocks, sems)
    rows[...] = jnp.zeros_like(rows)
    columns[...] = jnp.zeros_like(columns)
    faces_ref[...] = jnp.zeros_like(faces_ref)
    for e in range(elements):
        for copy in copies[e]:
            copy.wait()
        rows[:unknowns, :unknowns] = inv[e]
        fill_columns(e, depth, rhs, blocks, columns)
        whole[...] = stacked(left(rows[...]), columns[...])
        c_ref[e] = whole[:, :wide]
        bsn_ref[e] = left(whole[:, wide : wide + 2 * WIDE])
        bu_ref[e] = left(whole[:, wide + 2 * WIDE :])

        for f, kind in enumerate(("down", "high", "low")):
            at = f * WIDE
            for first, length in face_runs(kind):
                to, of = slice(at, at + length), slice(first, first + length)
                block = whole[of, :]
                for k in range(CORES):
                    faces_ref[k, e, to, :half] = block[:, k * half : (k + 1) * half]
                    faces_ref[k, e, to, half:] = block[:, wide:]
                at += length


def chip_blocks(faces_ref, fc_ref, fsn_ref, fu_ref, resp_ref, step_ref, held):
    elements, half = faces_ref.shape[1], fc_ref.shape[2]
    for e in range(CORES * elements):
        source = faces_ref.at[e // elements, e % elements]
        fc_ref[e] = source[:, :half]
        fsn_ref[e] = left(source[:, half : half + 2 * WIDE])
        own = source[:, half + 2 * WIDE :]
        fu_ref[e] = left(own)
        held[...] = -stacked(fu_ref[e], right(held[:WIDE, :])) if e else -own
        resp_ref[e] = left(held[...])
    step_ref[...] = held[:WIDE, :]


def halo_columns(s, n):
    return right(jnp.concatenate([padded(s, WIDE), padded(n, WIDE)], axis=0))


def first_faces(core_ref, fc_ref, fsn_ref, fu_ref, step_ref, *refs):
    halos, (q_ref, out_ref, held, sems) = refs[:4], refs[4:]
    elements = held.shape[2]
    copies = []
    for k, halo in enumerate(halos):
        for e in range(elements):
            copy = pltpu.make_async_copy(halo.at[e, :, 0, :], held.at[k // 2, k % 2, e], sems.at[k, e])
            copy.start()
            copies.append(copy)
    for copy in copies:
        copy.wait()
    half = fc_ref.shape[2]
    for e in range(CORES * elements):
        owner, of = divmod(e, elements)
        other = lax.rem(core_ref[0] + owner, 2)
        q = fc_ref[e] - stacked(fsn_ref[e], halo_columns(held[other, 0, of], held[other, 1, of]))
        if e:
            q = q - stacked(fu_ref[e], right(q_ref[e - 1, :WIDE, :]))
        q_ref[e] = q
    out_ref[:, :half] = q_ref[CORES * elements - 1, :WIDE, :]
    out_ref[:, half:] = step_ref[...]


def last_faces(core_ref, fc_ref, fsn_ref, fu_ref, below_ref, above_ref, q_ref, out_ref, away_ref):
    count = fc_ref.shape[0]
    elements = count // CORES
    for e in range(count):
        q = fc_ref[e, :WIDE, :] - stacked(fsn_ref[e, :WIDE, :], halo_columns(below_ref[e], above_ref[e]))
        if e:
            q = q - stacked(fu_ref[e, :WIDE, :], right(q_ref[e - 1]))
        q_ref[e] = q
    out_ref[...] = q_ref[count - 1]
    other = (1 - core_ref[0]) * elements
    for e in range(elements):
        away_ref[0, e] = below_ref[other + e]
        away_ref[1, e] = above_ref[other + e]


def through_chips(core_ref, inflow_ref, chips, steps):
    half = inflow_ref.shape[1]
    inflow_ref[...] = jnp.zeros_like(inflow_ref)
    for back in range(len(chips), 0, -1):

        @pl.when(core_ref[1] >= back)
        def _():
            passed = stacked(left(steps[back - 1][:, half:]), right(inflow_ref[...]))
            inflow_ref[...] = chips[back - 1][:, :half] + passed


def next_faces(core_ref, q_ref, resp_ref, *refs):
    high_ref, low_ref, inflow_ref = refs[-3:]
    through_chips(core_ref, inflow_ref, refs[:-3], refs[:-3])
    inflow = right(inflow_ref[...])
    for e in range(q_ref.shape[0]):
        faces = q_ref[e, WIDE:, :] + stacked(resp_ref[e, WIDE:, :], inflow)
        high_ref[e] = faces[:WIDE]
        low_ref[e] = faces[WIDE:]


def inflow_of_cores(core_ref, q_ref, resp_ref, *refs):
    keep_ref, send_ref = refs[-2:]
    count = (len(refs) - 2) // 2
    through_chips(core_ref, keep_ref, refs[:count], refs[count:-2])
    last = q_ref.shape[0] // CORES - 1

    @pl.when(core_ref[0] == 0)
    def _():
        send_ref[...] = q_ref[last] + stacked(resp_ref[last, :WIDE, :], right(keep_ref[...]))

    @pl.when(core_ref[0] == 1)
    def _():
        send_ref[...] = keep_ref[...]
        keep_ref[...] = q_ref[last] + stacked(resp_ref[last, :WIDE, :], right(send_ref[...]))


def join(core_ref, keep_ref, got_ref, inflow_ref):
    half = keep_ref.shape[1]

    @pl.when(core_ref[0] == 0)
    def _():
        inflow_ref[:, :half] = keep_ref[...]
        inflow_ref[:, half:] = got_ref[...]

    @pl.when(core_ref[0] == 1)
    def _():
        inflow_ref[:, :half] = got_ref[...]
        inflow_ref[:, half:] = keep_ref[...]


def field_without_inflow(core_ref, c_ref, bsn_ref, below_ref, above_ref, got_ref, p_ref, halo):
    elements, half = c_ref.shape[0], below_ref.shape[2]
    for e in range(elements):

        def place(own):
            mine, other = slice(own * half, (own + 1) * half), slice((1 - own) * half, (2 - own) * half)
            for k, ref in enumerate((below_ref, above_ref)):
                rows = slice(k * WIDE, (k + 1) * WIDE)
                halo[rows, mine] = ref[own * elements + e]
                halo[rows, other] = got_ref[k, e]

        for k in range(CORES):
            pl.when(core_ref[0] == k)(functools.partial(place, k))
        p_ref[e] = c_ref[e] - stacked(bsn_ref[e], right(halo[...]))


def whole_field(core_ref, p_ref, bu_ref, keep_ref, got_ref, out_ref, inflow_ref, held, sems):
    join(core_ref, keep_ref, got_ref, inflow_ref)
    elements, unknowns = held.shape[:2]
    copies = []
    for e in range(elements):
        if e:
            at = 0
            for first, length in face_runs("down"):
                inflow_ref[at : at + length, :] = held[e - 1, first : first + length, :]
                at += length
        value = p_ref[e] - stacked(bu_ref[e], right(inflow_ref[...]))
        held[e] = value[:unknowns]
        copy = pltpu.make_async_copy(held.at[e], out_ref.at[e, :, 0, :], sems.at[e])
        copy.start()
        copies.append(copy)
    for copy in copies:
        copy.wait()


def ring(axis, by):
    count = lax.axis_size(axis)
    return [(i, (i + by) % count) for i in range(count)]


def per_device(right_side, start_field, block_inverse, upwind_block, south_block, north_block):
    by_row = lambda x: x.transpose(0, 2, 1, 3)
    rhs, start, inverse, upwind, south, north = map(
        by_row, (right_side, start_field, block_inverse, upwind_block, south_block, north_block)
    )
    elements, unknowns, _, columns = rhs.shape
    depth = -(-unknowns // 128) * 128
    half = columns // CORES
    count = CORES * elements
    devices, spans = lax.axis_size("sweep"), lax.axis_size("span")
    place = lax.axis_index("sweep")
    where = jnp.stack([place % CORES, place // CORES]).astype(jnp.int32)
    dma = pltpu.SemaphoreType.DMA
    f32, bf16 = jnp.float32, jnp.bfloat16
    core = (SMEM, where)
    face = (elements, FACE, 1, half)

    def held(arrays):
        return [(VMEM, x) for x in arrays]

    def swap(x):
        return lax.ppermute(x, "sweep", [(i, i ^ 1) for i in range(devices)])

    def from_chips(x):
        return [
            lax.ppermute(x, "sweep", ring("sweep", CORES * back))
            for back in range(1, devices // CORES)
        ]

    def along_span(x, by, other_core):
        pairs = [
            (i * spans + j, (i ^ other_core) * spans + (j + by) % spans)
            for i in range(devices)
            for j in range(spans)
        ]
        return lax.ppermute(x, ("sweep", "span"), pairs)

    runs = start.reshape(elements, NODE**2, VARS * NODE, 1, columns)
    found = call(
        start_faces,
        [(VMEM, (elements, NODE**2, NODE, 1, half), f32)] * 4,
        core, (HBM, runs),
        scratch=[dma((4,))],
        limit=MOST,
    )
    found = [x.reshape(face) for x in found]
    halos = [along_span(found[k], -1 if k % 2 else 1, k // 2) for k in range(4)]
    c, bsn, bu, own = call(
        fold_blocks,
        [
            (VMEM, (elements, depth, columns), f32),
            (VMEM, (elements, depth, 6 * WIDE), bf16),
            (VMEM, (elements, depth, 3 * WIDE), bf16),
            (VMEM, (CORES, elements, 3 * WIDE, half + 3 * WIDE), f32),
        ],
        *[(HBM, x) for x in (inverse, rhs, upwind, south, north)],
        scratch=[
            VMEM((elements, unknowns, unknowns), f32),
            VMEM((elements, unknowns, columns), f32),
            VMEM((elements, 3, unknowns, FACE), f32),
            VMEM((depth, depth), f32),
            VMEM((3 * depth, columns + 3 * WIDE), bf16),
            VMEM((depth, columns + 3 * WIDE), f32),
            dma((elements, 5)),
        ],
        us=0,
        limit=MOST,
        after=found,
    )
    cores = lax.all_to_all(
        own, "sweep", 0, 0, axis_index_groups=[[i, i + 1] for i in range(0, devices, CORES)]
    )
    fc, fsn, fu, resp, step = call(
        chip_blocks,
        [
            (VMEM, (count, 3 * WIDE, half), f32),
            (VMEM, (count, 3 * WIDE, 6 * WIDE), bf16),
            (VMEM, (count, 3 * WIDE, 3 * WIDE), bf16),
            (VMEM, (count, 3 * WIDE, 3 * WIDE), bf16),
            (VMEM, (WIDE, WIDE), f32),
        ],
        (VMEM, cores),
        scratch=[VMEM((3 * WIDE, WIDE), f32)],
        us=0,
    )
    q, out = call(
        first_faces,
        [(VMEM, (count, 3 * WIDE, half), f32), (VMEM, (WIDE, half + WIDE), f32)],
        core, *held((fc, fsn, fu, step)), *[(HBM, x) for x in halos],
        scratch=[VMEM((2, 2, elements, FACE, half), f32), dma((4, elements))],
        us=2,
    )
    chips = from_chips(out)
    high, low = call(
        next_faces,
        [(VMEM, (count, WIDE, half), f32)] * 2,
        core, *held((q, resp, *chips)),
        scratch=[VMEM((WIDE, half), f32)],
        us=2,
    )
    below, above = along_span(high, 1, 0), along_span(low, -1, 0)
    q, out, away = call(
        last_faces,
        [
            (VMEM, (count, WIDE, half), f32),
            (VMEM, (WIDE, half), f32),
            (VMEM, (2, elements, WIDE, half), f32),
        ],
        core, *held((fc, fsn, fu, below, above)),
        us=1,
    )
    last_chips = from_chips(out)
    (part,) = call(
        field_without_inflow,
        [(VMEM, (elements, depth, columns), f32)],
        core, *held((c, bsn, below, above, swap(away))),
        scratch=[VMEM((2 * WIDE, columns), f32)],
        us=2,
    )
    keep, send = call(
        inflow_of_cores,
        [(VMEM, (WIDE, half), f32)] * 2,
        core, *held((q, resp, *last_chips, *chips)),
        after=[part],
    )
    (field,) = call(
        whole_field,
        [(HBM, rhs.shape, f32)],
        core, *held((part, bu, keep, swap(send))),
        scratch=[
            VMEM((WIDE, columns), f32),
            VMEM((elements, unknowns, columns), f32),
            dma((elements,)),
        ],
        us=2,
    )
    return by_row(field)


def solution(mesh):
    spec = P("sweep", "span", None, None)
    return jax.shard_map(
        per_device, mesh=mesh, in_specs=(spec,) * 6, out_specs=spec, check_vma=False
    )
```

```python
import functools

import jax
import jax.numpy as jnp
from jax import lax
from jax.experimental import pallas as pl
from jax.experimental.pallas import tpu as pltpu
from jax.sharding import PartitionSpec as P

VARS = 5
NODE = 5
FACE = VARS * NODE**2
WIDE = 128
SWEEPS = 2
CORES = 2
PANELS = 1
ORDER = (3, 1, 2, 0)
LIMIT = 24 * 1024 * 1024
MOST = 62 * 1024 * 1024
ANY = pl.ANY
HBM = pltpu.HBM
VMEM = pltpu.VMEM
SMEM = pltpu.SMEM


def face_runs(kind):
    if kind == "down":
        return [(var * NODE**3 + (NODE - 1) * NODE**2, NODE**2) for var in range(VARS)]
    b = NODE - 1 if kind == "high" else 0
    return [
        (var * NODE**3 + a * NODE**2 + b * NODE, NODE)
        for var in range(VARS)
        for a in range(NODE)
    ]


def split(x):
    top = x.astype(jnp.bfloat16)
    return top, (x - top.astype(jnp.float32)).astype(jnp.bfloat16)


def left(x):
    high, low = split(x)
    return jnp.concatenate([high, high, low], axis=1)


def right(x):
    high, low = split(x)
    return jnp.concatenate([high, low, high], axis=0)


def stacked(a, b):
    return jnp.dot(a, b, preferred_element_type=jnp.float32)


def padded(x, rows):
    short = rows - x.shape[0]
    return jnp.concatenate([x, jnp.zeros((short, x.shape[1]), x.dtype)], axis=0) if short else x


def call(kernel, outs, *args, scratch=(), us=1, after=(), limit=LIMIT, aliases=None):
    args = list(args) + [(ANY, x) for x in after]

    def body(*refs):
        given = len(args) - len(after)
        kernel(*refs[:given], *refs[len(args) :])

    return pl.pallas_call(
        body,
        out_shape=[jax.ShapeDtypeStruct(shape, kind) for _, shape, kind in outs],
        in_specs=[pl.BlockSpec(memory_space=space) for space, _ in args],
        out_specs=[pl.BlockSpec(memory_space=space) for space, _, _ in outs],
        scratch_shapes=list(scratch),
        input_output_aliases=aliases or {},
        compiler_params=pltpu.CompilerParams(vmem_limit_bytes=limit),
        cost_estimate=pl.CostEstimate(flops=int(us * 10**9), bytes_accessed=0, transcendentals=0),
        name=getattr(kernel, "func", kernel).__name__,
    )(*[array for _, array in args])


def start_faces(core_ref, field_ref, *refs):
    outs, sems = refs[:-1], refs[-1]
    half = outs[0].shape[-1]
    parts = []
    for k, out in enumerate(outs):
        own = core_ref[0] if k < 2 else 1 - core_ref[0]
        low = core_ref[2] if k % 2 == 0 else 1 - core_ref[2]
        part = pltpu.make_async_copy(
            field_ref.at[
                :, :, pl.ds((1 - low) * (NODE - 1) * NODE, NODE), :,
                pl.ds(pl.multiple_of(own * half, half), half),
            ],
            out,
            sems.at[k],
        )
        part.start()
        parts.append(part)
    for part in parts:
        part.wait()


def load_rows(pairs, sems):
    copies = []
    for k, (source, held) in enumerate(pairs):
        copies.append(pltpu.make_async_copy(source, held, sems.at[k]))
        copies[-1].start()
    return copies


def load_blocks(inv_ref, rhs_ref, up_ref, south_ref, north_ref, inv, rhs, blocks, sems):
    return [
        load_rows(
            [
                (inv_ref.at[e, :, 0, :], inv.at[e]),
                (rhs_ref.at[e, :, 0, :], rhs.at[e]),
                (south_ref.at[e, :, 0, :], blocks.at[e, 0]),
                (north_ref.at[e, :, 0, :], blocks.at[e, 1]),
                (up_ref.at[e, :, 0, :], blocks.at[e, 2]),
            ],
            sems.at[e],
        )
        for e in range(inv_ref.shape[0])
    ]


def fill_columns(e, depth, rhs, blocks, columns):
    wide = rhs.shape[2]
    columns[:, :wide] = right(padded(rhs[e], depth))
    for k in range(3):
        at = wide + k * WIDE
        block = right(padded(blocks[e, k], depth))
        columns[:, at : at + FACE] = block


def fold_faces(inv_ref, rhs_ref, up_ref, south_ref, north_ref, faces_ref,
               inv, rhs, blocks, rows, columns, sems):
    elements, depth, wide = inv.shape[0], rows.shape[1], rhs.shape[2]
    half = wide // CORES
    copies = load_blocks(inv_ref, rhs_ref, up_ref, south_ref, north_ref, inv, rhs, blocks, sems)
    rows[...] = jnp.zeros_like(rows)
    columns[...] = jnp.zeros_like(columns)
    for e in range(elements):
        copies[e][0].wait()
        for f, kind in enumerate(("down", "high", "low")):
            at = f * WIDE
            for first, length in face_runs(kind):
                rows[at : at + length, : inv.shape[2]] = inv[e, first : first + length, :]
                at += length
        for copy in copies[e][1:]:
            copy.wait()
        fill_columns(e, depth, rhs, blocks, columns)
        product = stacked(left(rows[...]), columns[...])
        for k in range(CORES):
            faces_ref[k, e, :, :half] = product[:, k * half : (k + 1) * half]
            faces_ref[k, e, :, half:] = product[:, wide:]


def fold_rows(inv_ref, rhs_ref, up_ref, south_ref, north_ref, c_ref, bsn_ref, bu_ref,
              inv, rhs, blocks, rows, columns, sems):
    elements, unknowns = inv.shape[:2]
    depth, wide = rows.shape[1], rhs.shape[2]
    copies = load_blocks(inv_ref, rhs_ref, up_ref, south_ref, north_ref, inv, rhs, blocks, sems)
    rows[...] = jnp.zeros_like(rows)
    columns[...] = jnp.zeros_like(columns)
    for e in range(elements):
        for copy in copies[e]:
            copy.wait()
        rows[:unknowns, :unknowns] = inv[e]
        fill_columns(e, depth, rhs, blocks, columns)
        product = stacked(left(rows[...]), columns[...])
        c_ref[e] = product[:, :wide]
        bsn_ref[e] = left(product[:, wide : wide + 2 * WIDE])
        bu_ref[e] = left(product[:, wide + 2 * WIDE :])


def chip_blocks(faces_ref, fc_ref, fsn_ref, fu_ref, resp_ref, step_ref, held):
    elements, half = faces_ref.shape[1], fc_ref.shape[2]
    for e in range(CORES * elements):
        source = faces_ref.at[e // elements, e % elements]
        fc_ref[e] = source[:, :half]
        fsn_ref[e] = left(source[:, half : half + 2 * WIDE])
        own = source[:, half + 2 * WIDE :]
        fu_ref[e] = left(own)
        held[...] = -stacked(fu_ref[e], right(held[:WIDE, :])) if e else -own
        resp_ref[e] = left(held[...])
    step_ref[...] = held[:WIDE, :]


def south_north(core_ref, k):
    return pl.multiple_of(((1 - core_ref[2]) if k == 0 else core_ref[2]) * WIDE, WIDE)


def first_traces(core_ref, fc_ref, fsn_ref, fu_ref, *refs):
    halos, (q_ref, out_ref, columns_ref, held, sems) = refs[:4], refs[4:]
    elements = held.shape[2]
    copies = []
    for k, halo in zip(ORDER, halos):
        north = 1 - core_ref[2] if k % 2 == 0 else core_ref[2]
        for e in range(elements):
            copy = pltpu.make_async_copy(halo.at[e, :, 0, :], held.at[k // 2, north, e], sems.at[k, e])
            copy.start()
            copies.append(copy)
    for copy in copies:
        copy.wait()
    for e in range(CORES * elements):
        owner, of = divmod(e, elements)
        other = lax.rem(core_ref[0] + owner, 2)
        both = [padded(held[other, k, of], WIDE) for k in range(2)]
        columns_ref[e] = right(jnp.concatenate(both, axis=0))
        q = fc_ref[e, :WIDE, :] - stacked(fsn_ref[e, :WIDE, :], columns_ref[e])
        if e:
            q = q - stacked(fu_ref[e, :WIDE, :], right(q_ref[e - 1]))
        q_ref[e] = q
    out_ref[...] = q_ref[CORES * elements - 1]


def other_faces(fc_ref, fsn_ref, fu_ref, columns_ref, q_ref, faces_ref):
    for e in range(fc_ref.shape[0]):
        faces = fc_ref[e, WIDE:, :] - stacked(fsn_ref[e, WIDE:, :], columns_ref[e])
        if e:
            faces = faces - stacked(fu_ref[e, WIDE:, :], right(q_ref[e - 1]))
        faces_ref[e] = faces


def last_faces(panel, core_ref, fc_ref, fsn_ref, fu_ref, first_ref, second_ref, q_ref, out_ref, away_ref, halo):
    count, width = fc_ref.shape[0], q_ref.shape[2]
    elements = count // CORES
    for e in range(count):
        for k, ref in enumerate((first_ref, second_ref)):
            halo[pl.ds(south_north(core_ref, k), WIDE), :] = ref[e]
        q = fc_ref[e, :WIDE, panel * width : (panel + 1) * width]
        q = q - stacked(fsn_ref[e, :WIDE, :], right(halo[...]))
        if e:
            q = q - stacked(fu_ref[e, :WIDE, :], right(q_ref[e - 1]))
        q_ref[e] = q
    out_ref[...] = q_ref[count - 1]
    other = (1 - core_ref[0]) * elements
    for e in range(elements):
        away_ref[0, e] = first_ref[other + e]
        away_ref[1, e] = second_ref[other + e]


def through_chips(core_ref, inflow_ref, chips, steps):
    inflow_ref[...] = jnp.zeros_like(inflow_ref)
    for back in range(len(chips), 0, -1):

        @pl.when(core_ref[1] >= back)
        def _():
            if back == len(chips):
                inflow_ref[...] = chips[back - 1][...]
            else:
                passed = stacked(left(steps[back - 1][...]), right(inflow_ref[...]))
                inflow_ref[...] = chips[back - 1][...] + passed


def next_faces(panel, core_ref, faces_ref, resp_ref, *refs):
    first_ref, second_ref, inflow_ref, both = refs[-4:]
    width = inflow_ref.shape[1]
    count = (len(refs) - 3) // 2
    through_chips(core_ref, inflow_ref, refs[:count], refs[count:-4])
    inflow = right(inflow_ref[...])
    first = pl.multiple_of(core_ref[2] * WIDE, WIDE)
    second = pl.multiple_of((1 - core_ref[2]) * WIDE, WIDE)
    for e in range(faces_ref.shape[0]):
        both[...] = faces_ref[e, :, panel * width : (panel + 1) * width] + stacked(resp_ref[e, WIDE:, :], inflow)
        first_ref[e] = both[pl.ds(first, WIDE), :]
        second_ref[e] = both[pl.ds(second, WIDE), :]


def inflow_of_cores(core_ref, q_ref, resp_ref, *refs):
    keep_ref, send_ref = refs[-2:]
    count = (len(refs) - 1) // 2
    through_chips(core_ref, keep_ref, refs[:count], refs[count:-2])
    last = q_ref.shape[0] // CORES - 1

    @pl.when(core_ref[0] == 0)
    def _():
        send_ref[...] = q_ref[last] + stacked(resp_ref[last, :WIDE, :], right(keep_ref[...]))

    @pl.when(core_ref[0] == 1)
    def _():
        send_ref[...] = keep_ref[...]
        keep_ref[...] = q_ref[last] + stacked(resp_ref[last, :WIDE, :], right(send_ref[...]))


def join(core_ref, keep_ref, got_ref, inflow_ref):
    half = keep_ref.shape[1]

    @pl.when(core_ref[0] == 0)
    def _():
        inflow_ref[:, :half] = keep_ref[...]
        inflow_ref[:, half:] = got_ref[...]

    @pl.when(core_ref[0] == 1)
    def _():
        inflow_ref[:, :half] = got_ref[...]
        inflow_ref[:, half:] = keep_ref[...]


def field_without_inflow(panel, core_ref, c_ref, bsn_ref, first_ref, second_ref, got_ref, p_ref, halo):
    elements, width = c_ref.shape[0], first_ref.shape[2]
    half = c_ref.shape[2] // CORES
    for e in range(elements):

        def place(own):
            mine = slice(own * width, (own + 1) * width)
            other = slice((1 - own) * width, (2 - own) * width)
            for k, ref in enumerate((first_ref, second_ref)):
                rows = pl.ds(south_north(core_ref, k), WIDE)
                halo[rows, mine] = ref[own * elements + e]
                halo[rows, other] = got_ref[k, e]

        for k in range(CORES):
            pl.when(core_ref[0] == k)(functools.partial(place, k))
        change = stacked(bsn_ref[e], right(halo[...]))
        for k in range(CORES):
            at = k * half + panel * width
            p_ref[e, :, k * width : (k + 1) * width] = (
                c_ref[e, :, at : at + width] - change[:, k * width : (k + 1) * width]
            )


def whole_field(panel, core_ref, p_ref, bu_ref, keep_ref, got_ref, *refs):
    out_ref, inflow_ref, held, sems = refs[-4:]
    join(core_ref, keep_ref, got_ref, inflow_ref)
    elements, unknowns = held.shape[:2]
    width = keep_ref.shape[1]
    half = out_ref.shape[3] // CORES
    copies = []
    for e in range(elements):
        if e:
            at = 0
            for first, length in face_runs("down"):
                inflow_ref[at : at + length, :] = held[e - 1, first : first + length, :]
                at += length
        value = p_ref[e] - stacked(bu_ref[e], right(inflow_ref[...]))
        held[e] = value[:unknowns]
        for k in range(CORES):
            copy = pltpu.make_async_copy(
                held.at[e, :, pl.ds(k * width, width)],
                out_ref.at[e, :, 0, pl.ds(k * half + panel * width, width)],
                sems.at[e, k],
            )
            copy.start()
            copies.append(copy)
    for copy in copies:
        copy.wait()


def ring(axis, by):
    count = lax.axis_size(axis)
    return [(i, (i + by) % count) for i in range(count)]


def per_device(right_side, start_field, block_inverse, upwind_block, south_block, north_block):
    by_row = lambda x: x.transpose(0, 2, 1, 3)
    rhs, start, inverse, upwind, south, north = map(
        by_row, (right_side, start_field, block_inverse, upwind_block, south_block, north_block)
    )
    elements, unknowns, _, columns = rhs.shape
    depth = -(-unknowns // 128) * 128
    half = columns // CORES
    width = half // PANELS
    count = CORES * elements
    devices, spans = lax.axis_size("sweep"), lax.axis_size("span")
    place = lax.axis_index("sweep")
    odd = lax.axis_index("span") % 2
    where = jnp.stack([place % CORES, place // CORES, odd]).astype(jnp.int32)
    dma = pltpu.SemaphoreType.DMA
    f32, bf16 = jnp.float32, jnp.bfloat16
    core = (SMEM, where)
    face = (elements, FACE, 1, half)

    def held(arrays):
        return [(VMEM, x) for x in arrays]

    def swap(x):
        return lax.ppermute(x, "sweep", [(i, i ^ 1) for i in range(devices)])

    def from_chips(x):
        return [
            lax.ppermute(x, "sweep", ring("sweep", CORES * back))
            for back in range(1, devices // CORES)
        ]

    def along_span(x, second, other_core):
        pairs = []
        for i in range(devices):
            for j in range(spans):
                by = 1 if (j + second) % 2 == 0 else -1
                pairs.append((i * spans + j, (i ^ other_core) * spans + (j + by) % spans))
        return lax.ppermute(x, ("sweep", "span"), pairs)

    runs = start.reshape(elements, NODE**2, VARS * NODE, 1, columns)
    found = call(
        start_faces,
        [(VMEM, (elements, NODE**2, NODE, 1, half), f32)] * 4,
        core, (HBM, runs),
        scratch=[dma((4,))],
    )
    halos = [along_span(found[k].reshape(face), k % 2, k // 2) for k in range(4)]
    raw = [(HBM, x) for x in (inverse, rhs, upwind, south, north)]
    raw_scratch = [
        VMEM((elements, unknowns, unknowns), f32),
        VMEM((elements, unknowns, columns), f32),
        VMEM((elements, 3, unknowns, FACE), f32),
    ]
    fold_scratch = [VMEM((3 * depth, columns + 3 * WIDE), bf16), dma((elements, 5))]
    (own,) = call(
        fold_faces,
        [(VMEM, (CORES, elements, 3 * WIDE, half + 3 * WIDE), f32)],
        *raw,
        scratch=raw_scratch + [VMEM((3 * WIDE, depth), f32)] + fold_scratch,
        us=0,
        limit=MOST,
        after=found,
    )
    cores = lax.all_to_all(
        own, "sweep", 0, 0, axis_index_groups=[[i, i + 1] for i in range(0, devices, CORES)]
    )
    fc, fsn, fu, resp, step = call(
        chip_blocks,
        [
            (VMEM, (count, 3 * WIDE, half), f32),
            (VMEM, (count, 3 * WIDE, 6 * WIDE), bf16),
            (VMEM, (count, 3 * WIDE, 3 * WIDE), bf16),
            (VMEM, (count, 3 * WIDE, 3 * WIDE), bf16),
            (VMEM, (WIDE, WIDE), f32),
        ],
        (VMEM, cores),
        scratch=[VMEM((3 * WIDE, WIDE), f32)],
        us=0,
    )
    steps = from_chips(step)[:-1]
    q, out, halo_stack = call(
        first_traces,
        [
            (VMEM, (count, WIDE, half), f32),
            (VMEM, (WIDE, half), f32),
            (VMEM, (count, 6 * WIDE, half), bf16),
        ],
        core, *held((fc, fsn, fu)), *[(HBM, halos[k]) for k in ORDER],
        scratch=[VMEM((2, 2, elements, FACE, half), f32), dma((4, elements))],
        us=2,
    )
    chips = [from_chips(out)]
    (faces,) = call(
        other_faces,
        [(VMEM, (count, 2 * WIDE, half), f32)],
        *held((fc, fsn, fu, halo_stack, q)),
        us=2,
        after=steps,
    )
    halos, last = [], []
    for p in range(PANELS):
        last = call(
            functools.partial(next_faces, p),
            [(VMEM, (count, WIDE, width), f32)] * 2,
            core, *held((faces, resp, *chips[p], *steps)),
            scratch=[VMEM((WIDE, width), f32), VMEM((2 * WIDE, width), f32)],
            us=1,
            after=last,
        )
        halos.append([along_span(last[k], k, 0) for k in range(2)])
    c, bsn, bu = call(
        fold_rows,
        [
            (VMEM, (elements, depth, columns), f32),
            (VMEM, (elements, depth, 6 * WIDE), bf16),
            (VMEM, (elements, depth, 3 * WIDE), bf16),
        ],
        *raw,
        scratch=raw_scratch + [VMEM((depth, depth), f32)] + fold_scratch,
        us=10,
        after=last,
    )
    field, last = None, [c]
    for p in range(PANELS):
        q, out, away = call(
            functools.partial(last_faces, p),
            [
                (VMEM, (count, WIDE, width), f32),
                (VMEM, (WIDE, width), f32),
                (VMEM, (2, elements, WIDE, width), f32),
            ],
            core, *held((fc, fsn, fu, *halos[p])),
            scratch=[VMEM((2 * WIDE, width), f32)],
            us=1,
            after=last,
        )
        last = [out]
        last_chips = from_chips(out)
        (part,) = call(
            functools.partial(field_without_inflow, p),
            [(VMEM, (elements, depth, CORES * width), f32)],
            core, *held((c, bsn, *halos[p], swap(away))),
            scratch=[VMEM((2 * WIDE, CORES * width), f32)],
            us=1,
        )
        keep, send = call(
            inflow_of_cores,
            [(VMEM, (WIDE, width), f32)] * 2,
            core, *held((q, resp, *last_chips, *steps)),
            after=[part],
        )
        before = [] if field is None else [(HBM, field)]
        (field,) = call(
            functools.partial(whole_field, p),
            [(HBM, rhs.shape, f32)],
            core, *held((part, bu, keep, swap(send))), *before,
            scratch=[
                VMEM((WIDE, CORES * width), f32),
                VMEM((elements, unknowns, CORES * width), f32),
                dma((elements, CORES)),
            ],
            us=1,
            aliases={5: 0} if before else None,
        )
    return by_row(field)


def solution(mesh):
    spec = P("sweep", "span", None, None)
    return jax.shard_map(
        per_device, mesh=mesh, in_specs=(spec,) * 6, out_specs=spec, check_vma=False
    )
```

```python
import functools

import jax
import jax.numpy as jnp
from jax import lax
from jax.experimental import pallas as pl
from jax.experimental.pallas import tpu as pltpu
from jax.sharding import PartitionSpec as P

VARS = 5
NODE = 5
FACE = VARS * NODE**2
WIDE = 128
SWEEPS = 2
CORES = 2
ORDER = (3, 1, 2, 0)
LIMIT = 24 * 1024 * 1024
MOST = 60 * 1024 * 1024
ANY = pl.ANY
HBM = pltpu.HBM
VMEM = pltpu.VMEM
SMEM = pltpu.SMEM


def face_runs(kind):
    if kind == "down":
        return [(var * NODE**3 + (NODE - 1) * NODE**2, NODE**2) for var in range(VARS)]
    b = NODE - 1 if kind == "high" else 0
    return [
        (var * NODE**3 + a * NODE**2 + b * NODE, NODE)
        for var in range(VARS)
        for a in range(NODE)
    ]


def split(x):
    top = x.astype(jnp.bfloat16)
    return top, (x - top.astype(jnp.float32)).astype(jnp.bfloat16)


def left(x):
    high, low = split(x)
    return jnp.concatenate([high, high, low], axis=1)


def right(x):
    high, low = split(x)
    return jnp.concatenate([high, low, high], axis=0)


def stacked(a, b):
    return jnp.dot(a, b, preferred_element_type=jnp.float32)


def padded(x, rows):
    short = rows - x.shape[0]
    return jnp.concatenate([x, jnp.zeros((short, x.shape[1]), x.dtype)], axis=0) if short else x


def call(kernel, outs, *args, scratch=(), us=1, after=(), limit=LIMIT, aliases=None):
    args = list(args) + [(ANY, x) for x in after]

    def body(*refs):
        given = len(args) - len(after)
        kernel(*refs[:given], *refs[len(args) :])

    return pl.pallas_call(
        body,
        out_shape=[jax.ShapeDtypeStruct(shape, kind) for _, shape, kind in outs],
        in_specs=[pl.BlockSpec(memory_space=space) for space, _ in args],
        out_specs=[pl.BlockSpec(memory_space=space) for space, _, _ in outs],
        scratch_shapes=list(scratch),
        input_output_aliases=aliases or {},
        compiler_params=pltpu.CompilerParams(vmem_limit_bytes=limit),
        cost_estimate=pl.CostEstimate(flops=int(us * 10**9), bytes_accessed=0, transcendentals=0),
        name=getattr(kernel, "func", kernel).__name__,
    )(*[array for _, array in args])


def start_faces(core_ref, field_ref, *refs):
    outs, sems = refs[:-1], refs[-1]
    half = outs[0].shape[-1]
    parts = []
    for k, out in enumerate(outs):
        own = core_ref[0] if k < 2 else 1 - core_ref[0]
        low = core_ref[2] if k % 2 == 0 else 1 - core_ref[2]
        part = pltpu.make_async_copy(
            field_ref.at[
                :, :, pl.ds((1 - low) * (NODE - 1) * NODE, NODE), :,
                pl.ds(pl.multiple_of(own * half, half), half),
            ],
            out,
            sems.at[k],
        )
        part.start()
        parts.append(part)
    for part in parts:
        part.wait()


def load_rows(pairs, sems):
    copies = []
    for k, (source, held) in enumerate(pairs):
        copies.append(pltpu.make_async_copy(source, held, sems.at[k]))
        copies[-1].start()
    return copies


def load_blocks(inv_ref, rhs_ref, up_ref, south_ref, north_ref, inv, rhs, blocks, sems):
    return [
        load_rows(
            [
                (inv_ref.at[e, :, 0, :], inv.at[e]),
                (rhs_ref.at[e, :, 0, :], rhs.at[e]),
                (south_ref.at[e, :, 0, :], blocks.at[e, 0]),
                (north_ref.at[e, :, 0, :], blocks.at[e, 1]),
                (up_ref.at[e, :, 0, :], blocks.at[e, 2]),
            ],
            sems.at[e],
        )
        for e in range(inv_ref.shape[0])
    ]


def fill_columns(e, depth, rhs, blocks, columns):
    wide = rhs.shape[2]
    columns[:, :wide] = right(padded(rhs[e], depth))
    for k in range(3):
        at = wide + k * WIDE
        block = right(padded(blocks[e, k], depth))
        columns[:, at : at + FACE] = block


def fold_faces(inv_ref, rhs_ref, up_ref, south_ref, north_ref, faces_ref,
               inv, rhs, blocks, rows, columns, sems):
    elements, depth, wide = inv.shape[0], rows.shape[1], rhs.shape[2]
    half = wide // CORES
    copies = load_blocks(inv_ref, rhs_ref, up_ref, south_ref, north_ref, inv, rhs, blocks, sems)
    rows[...] = jnp.zeros_like(rows)
    columns[...] = jnp.zeros_like(columns)
    for e in range(elements):
        copies[e][0].wait()
        for f, kind in enumerate(("down", "high", "low")):
            at = f * WIDE
            for first, length in face_runs(kind):
                rows[at : at + length, : inv.shape[2]] = inv[e, first : first + length, :]
                at += length
        for copy in copies[e][1:]:
            copy.wait()
        fill_columns(e, depth, rhs, blocks, columns)
        product = stacked(left(rows[...]), columns[...])
        for k in range(CORES):
            faces_ref[k, e, :, :half] = product[:, k * half : (k + 1) * half]
            faces_ref[k, e, :, half:] = product[:, wide:]


def fold_element(e, raw, outs, inv, rhs, blocks, rows, columns, sems):
    inv_ref, rhs_ref, up_ref, south_ref, north_ref = raw
    unknowns = inv.shape[1]
    depth, wide = rows.shape[1], rhs.shape[2]
    copies = load_rows(
        [
            (inv_ref.at[e, :, 0, :], inv.at[0]),
            (rhs_ref.at[e, :, 0, :], rhs.at[0]),
            (south_ref.at[e, :, 0, :], blocks.at[0, 0]),
            (north_ref.at[e, :, 0, :], blocks.at[0, 1]),
            (up_ref.at[e, :, 0, :], blocks.at[0, 2]),
        ],
        sems,
    )
    rows[...] = jnp.zeros_like(rows)
    columns[...] = jnp.zeros_like(columns)
    for copy in copies:
        copy.wait()
    rows[:unknowns, :unknowns] = inv[0]
    fill_columns(0, depth, rhs, blocks, columns)
    product = stacked(left(rows[...]), columns[...])
    c_ref, bsn_ref, bu_ref = outs
    c_ref[...] = product[:, :wide]
    bsn_ref[...] = left(product[:, wide : wide + 2 * WIDE])
    bu_ref[...] = left(product[:, wide + 2 * WIDE :])


def fold_rest(core_ref, *refs):
    raw, scratch = refs[:5], refs[-6:]
    outs = refs[5:-6]
    for e in range(len(outs) // 3 - 1, -1, -1):
        one = functools.partial(fold_element, e, raw, outs[3 * e : 3 * e + 3], *scratch)
        if e:
            one()
        else:
            pl.when(core_ref[0] == 1)(one)


def chip_blocks(faces_ref, fc_ref, fsn_ref, fu_ref, resp_ref, step_ref, const_ref, high_ref, low_ref, held):
    elements, half = faces_ref.shape[1], fc_ref.shape[2]
    count = CORES * elements
    for e in range(count):
        source = faces_ref.at[e // elements, e % elements]
        fc_ref[e] = source[:, :half]
        fsn_ref[e] = left(source[:, half : half + 2 * WIDE])
        own = source[:, half + 2 * WIDE :]
        fu_ref[e] = left(own)
        held[...] = -stacked(fu_ref[e], right(held[:WIDE, :])) if e else -own
        resp_ref[e] = left(held[...])
    step_ref[...] = held[:WIDE, :]
    high_ref[WIDE:, elements * 2 * WIDE :] = jnp.zeros_like(high_ref[WIDE:, elements * 2 * WIDE :])
    low_ref[WIDE:, elements * 2 * WIDE :] = jnp.zeros_like(low_ref[WIDE:, elements * 2 * WIDE :])
    for rows, last in ((slice(0, WIDE), count - 1), (slice(WIDE, 2 * WIDE), elements - 1)):
        passed = None
        for e in range(last, -1, -1):
            source = faces_ref.at[e // elements, e % elements]
            block = source[:WIDE, :]
            value = block if passed is None else stacked(left(passed), right(block))
            const = value[:, :half] if passed is None else const + value[:, :half]
            at = slice(e * 2 * WIDE, (e + 1) * 2 * WIDE)
            high_ref[rows, at], low_ref[rows, at] = split(value[:, half : half + 2 * WIDE])
            passed = -value[:, half + 2 * WIDE :]
        const_ref[rows, :] = const


def south_north(core_ref, k):
    return pl.multiple_of(((1 - core_ref[2]) if k == 0 else core_ref[2]) * WIDE, WIDE)


def traces(const, high, low, halo_high, halo_low):
    dot = functools.partial(jnp.dot, preferred_element_type=jnp.float32)
    return const - (dot(high, halo_high) + (dot(high, halo_low) + dot(low, halo_high)))


def first_traces(core_ref, const_ref, high_ref, low_ref, *refs):
    halos, raw, (out_ref, halo_high, halo_low), outs = refs[:4], refs[4:9], refs[9:12], refs[12:15]
    held, sems, scratch = refs[15], refs[16], refs[17:]
    elements = held.shape[1]
    copies = load_rows([(halo.at[:, :, 0, :], held.at[k]) for k, halo in enumerate(halos)], sems)
    for k, kind in enumerate(ORDER):
        copies[k].wait()
        owner = core_ref[0] if kind < 2 else 1 - core_ref[0]
        for e in range(elements):
            row = 2 * WIDE * (owner * elements + e) + south_north(core_ref, kind % 2)
            at = pl.ds(pl.multiple_of(row, WIDE), WIDE)
            halo_high[at, :], halo_low[at, :] = split(padded(held[k, e], WIDE))
    out_ref[...] = traces(
        const_ref[:WIDE, :], high_ref[:WIDE, :], low_ref[:WIDE, :], halo_high[...], halo_low[...]
    )
    pl.when(core_ref[0] == 0)(functools.partial(fold_element, 0, raw, outs, *scratch))


def other_faces(fc_ref, fsn_ref, fu_ref, halo_high, halo_low, faces_ref):
    trace = None
    for e in range(fc_ref.shape[0]):
        at = slice(2 * e * WIDE, 2 * (e + 1) * WIDE)
        high = halo_high[at, :]
        faces = fc_ref[e] - stacked(fsn_ref[e], jnp.concatenate([high, halo_low[at, :], high], axis=0))
        if e:
            faces = faces - stacked(fu_ref[e], right(trace))
        trace = faces[:WIDE]
        faces_ref[e] = faces[WIDE:]


def last_traces(core_ref, const_ref, high_ref, low_ref, second_ref, first_ref, out_ref, lead_ref, away_ref,
                halo_high, halo_low):
    count = first_ref.shape[0]
    elements = count // CORES
    for e in range(count):
        for k, ref in enumerate((first_ref, second_ref)):
            at = pl.ds(pl.multiple_of(south_north(core_ref, k) + 2 * e * WIDE, WIDE), WIDE)
            halo_high[at, :], halo_low[at, :] = split(ref[e])
    both = traces(const_ref[...], high_ref[...], low_ref[...], halo_high[...], halo_low[...])
    out_ref[...] = both[:WIDE]
    lead_ref[...] = both[WIDE:]
    other = (1 - core_ref[0]) * elements
    for e in range(elements):
        away_ref[0, e] = first_ref[other + e]
        away_ref[1, e] = second_ref[other + e]


def through_chips(core_ref, inflow_ref, chips, steps):
    inflow_ref[...] = jnp.zeros_like(inflow_ref)
    for back in range(len(chips), 0, -1):

        @pl.when(core_ref[1] >= back)
        def _():
            if back == len(chips):
                inflow_ref[...] = chips[back - 1][...]
            else:
                passed = stacked(left(steps[back - 1][...]), right(inflow_ref[...]))
                inflow_ref[...] = chips[back - 1][...] + passed


def next_faces(core_ref, faces_ref, resp_ref, *refs):
    first_ref, second_ref, inflow_ref, both = refs[-4:]
    count = (len(refs) - 3) // 2
    through_chips(core_ref, inflow_ref, refs[:count], refs[count:-4])
    inflow = right(inflow_ref[...])
    first = pl.multiple_of(core_ref[2] * WIDE, WIDE)
    second = pl.multiple_of((1 - core_ref[2]) * WIDE, WIDE)
    for e in range(faces_ref.shape[0]):
        both[e] = faces_ref[e] + stacked(resp_ref[e, WIDE:, :], inflow)
    for e in range(faces_ref.shape[0]):
        first_ref[e] = both[e, pl.ds(first, WIDE), :]
        second_ref[e] = both[e, pl.ds(second, WIDE), :]


def inflow_of_cores(core_ref, lead_ref, resp_ref, *refs):
    keep_ref, send_ref = refs[-2:]
    count = (len(refs) - 1) // 2
    through_chips(core_ref, keep_ref, refs[:count], refs[count:-2])
    last = resp_ref.shape[0] // CORES - 1

    @pl.when(core_ref[0] == 0)
    def _():
        send_ref[...] = lead_ref[...] + stacked(resp_ref[last, :WIDE, :], right(keep_ref[...]))

    @pl.when(core_ref[0] == 1)
    def _():
        send_ref[...] = keep_ref[...]
        keep_ref[...] = lead_ref[...] + stacked(resp_ref[last, :WIDE, :], right(send_ref[...]))


def join(core_ref, keep_ref, got_ref, inflow_ref):
    half = keep_ref.shape[1]

    @pl.when(core_ref[0] == 0)
    def _():
        inflow_ref[:, :half] = keep_ref[...]
        inflow_ref[:, half:] = got_ref[...]

    @pl.when(core_ref[0] == 1)
    def _():
        inflow_ref[:, :half] = got_ref[...]
        inflow_ref[:, half:] = keep_ref[...]


def field_without_inflow(other, core_ref, *refs):
    first_ref, second_ref, p_ref, halo = refs[-4:]
    elements, half = p_ref.shape[0], p_ref.shape[2]
    c_refs, bsn_refs = refs[: elements + 1], refs[elements + 1 : 2 * elements + 2]
    own = 0 if other else core_ref[0] * elements
    at = pl.ds(pl.multiple_of((1 - core_ref[0] if other else core_ref[0]) * half, half), half)
    for e in range(elements):
        for k, ref in enumerate((first_ref, second_ref)):
            halo[pl.ds(south_north(core_ref, k), WIDE), :] = ref[own + e]
        halos = right(halo[...])

        def place(c_ref, bsn_ref):
            p_ref[e] = c_ref[:, at] - stacked(bsn_ref[...], halos)

        by_core(core_ref, e, place, c_refs, bsn_refs)


def by_core(core_ref, e, use, *stacks):
    if e:
        use(*[refs[e + 1] for refs in stacks])
    else:
        for k in range(CORES):
            pl.when(core_ref[0] == k)(functools.partial(use, *[refs[k] for refs in stacks]))


def whole_field(core_ref, own_ref, other_ref, keep_ref, got_ref, *refs):
    bu_refs, (out_ref, inflow_ref, held, sems) = refs[:-4], refs[-4:]
    join(core_ref, keep_ref, got_ref, inflow_ref)
    elements, unknowns = held.shape[:2]
    half = keep_ref.shape[1]
    copies = []
    for e in range(elements):
        if e:
            at = 0
            for first, length in face_runs("down"):
                inflow_ref[at : at + length, :] = held[e - 1, first : first + length, :]
                at += length
        inflow = right(inflow_ref[...])

        def place(own, bu_ref):
            change = stacked(bu_ref[...], inflow)[:unknowns]
            for k in range(CORES):
                part = own_ref if k == own else other_ref
                at = slice(k * half, (k + 1) * half)
                held[e, :, at] = part[e, :unknowns, :] - change[:, at]

        for k in range(CORES):
            pl.when(core_ref[0] == k)(functools.partial(place, k, bu_refs[e + 1 if e else k]))
        copy = pltpu.make_async_copy(held.at[e], out_ref.at[e, :, 0, :], sems.at[e])
        copy.start()
        copies.append(copy)
    for copy in copies:
        copy.wait()


def ring(axis, by):
    count = lax.axis_size(axis)
    return [(i, (i + by) % count) for i in range(count)]


def per_device(right_side, start_field, block_inverse, upwind_block, south_block, north_block):
    by_row = lambda x: x.transpose(0, 2, 1, 3)
    rhs, start, inverse, upwind, south, north = map(
        by_row, (right_side, start_field, block_inverse, upwind_block, south_block, north_block)
    )
    elements, unknowns, _, columns = rhs.shape
    depth = -(-unknowns // 128) * 128
    half = columns // CORES
    count = CORES * elements
    devices, spans = lax.axis_size("sweep"), lax.axis_size("span")
    place = lax.axis_index("sweep")
    odd = lax.axis_index("span") % 2
    where = jnp.stack([place % CORES, place // CORES, odd]).astype(jnp.int32)
    dma = pltpu.SemaphoreType.DMA
    f32, bf16 = jnp.float32, jnp.bfloat16
    core = (SMEM, where)
    face = (elements, FACE, 1, half)

    def held(arrays):
        return [(VMEM, x) for x in arrays]

    def swap(x):
        return lax.ppermute(x, "sweep", [(i, i ^ 1) for i in range(devices)])

    def from_chips(x):
        return [
            lax.ppermute(x, "sweep", ring("sweep", CORES * back))
            for back in range(1, devices // CORES)
        ]

    def along_span(x, second, other_core):
        pairs = []
        for i in range(devices):
            for j in range(spans):
                by = 1 if (j + second) % 2 == 0 else -1
                pairs.append((i * spans + j, (i ^ other_core) * spans + (j + by) % spans))
        return lax.ppermute(x, ("sweep", "span"), pairs)

    runs = start.reshape(elements, NODE**2, VARS * NODE, 1, columns)
    found = call(
        start_faces,
        [(VMEM, (elements, NODE**2, NODE, 1, half), f32)] * 4,
        core, (HBM, runs),
        scratch=[dma((4,))],
    )
    halos = [along_span(found[k].reshape(face), k % 2, k // 2) for k in range(4)]
    raw = [(HBM, x) for x in (inverse, rhs, upwind, south, north)]
    raw_scratch = [
        VMEM((elements, unknowns, unknowns), f32),
        VMEM((elements, unknowns, columns), f32),
        VMEM((elements, 3, unknowns, FACE), f32),
    ]
    fold_scratch = [VMEM((3 * depth, columns + 3 * WIDE), bf16), dma((elements, 5))]
    (own,) = call(
        fold_faces,
        [(VMEM, (CORES, elements, 3 * WIDE, half + 3 * WIDE), f32)],
        *raw,
        scratch=raw_scratch + [VMEM((3 * WIDE, depth), f32)] + fold_scratch,
        us=0,
        limit=MOST,
        after=found,
    )
    cores = lax.all_to_all(
        own, "sweep", 0, 0, axis_index_groups=[[i, i + 1] for i in range(0, devices, CORES)]
    )
    fc, fsn, fu, resp, step, *trace_blocks = call(
        chip_blocks,
        [
            (VMEM, (count, 3 * WIDE, half), f32),
            (VMEM, (count, 3 * WIDE, 6 * WIDE), bf16),
            (VMEM, (count, 3 * WIDE, 3 * WIDE), bf16),
            (VMEM, (count, 3 * WIDE, 3 * WIDE), bf16),
            (VMEM, (WIDE, WIDE), f32),
            (VMEM, (2 * WIDE, half), f32),
        ]
        + [(VMEM, (2 * WIDE, 2 * count * WIDE), bf16)] * 2,
        (VMEM, cores),
        scratch=[VMEM((3 * WIDE, WIDE), f32)],
        us=0,
    )
    steps = from_chips(step)[:-1]
    halo_split = (2 * count * WIDE, half)
    folded = [
        (VMEM, (depth, columns), f32),
        (VMEM, (depth, 6 * WIDE), bf16),
        (VMEM, (depth, 3 * WIDE), bf16),
    ]
    one_scratch = [VMEM((1,) + x.shape[1:], f32) for x in raw_scratch]
    one_scratch += [VMEM((depth, depth), f32), VMEM((3 * depth, columns + 3 * WIDE), bf16), dma((5,))]
    out, *halo_parts = call(
        first_traces,
        [(VMEM, (WIDE, half), f32)] + [(VMEM, halo_split, bf16)] * 2 + folded,
        core, *held(trace_blocks), *[(HBM, halos[k]) for k in ORDER], *raw,
        scratch=[VMEM((4, elements, FACE, half), f32), dma((4,))] + one_scratch,
        us=2,
    )
    halo_parts, early = halo_parts[:2], halo_parts[2:]
    chips = from_chips(out)
    (faces,) = call(
        other_faces,
        [(VMEM, (count, 2 * WIDE, half), f32)],
        *held((fc, fsn, fu, *halo_parts)),
        us=2,
        after=steps,
    )
    last = call(
        next_faces,
        [(VMEM, (count, WIDE, half), f32)] * 2,
        core, *held((faces, resp, *chips, *steps)),
        scratch=[VMEM((WIDE, half), f32), VMEM((count, 2 * WIDE, half), f32)],
        us=1,
    )
    halos = [along_span(last[k], k, 0) for k in (1, 0)][::-1]
    late = call(
        fold_rest,
        folded * elements,
        core, *raw,
        scratch=one_scratch,
        us=10,
        after=last,
    )
    c, bsn, bu = [held([early[k], *late[k::3]]) for k in range(3)]
    out, lead, away = call(
        last_traces,
        [
            (VMEM, (WIDE, half), f32),
            (VMEM, (WIDE, half), f32),
            (VMEM, (2, elements, WIDE, half), f32),
        ],
        core, *held((*trace_blocks, *halos[::-1])),
        scratch=[VMEM(halo_split, bf16)] * 2,
        us=1,
        after=late[:1],
    )
    chips = from_chips(out)
    got = swap(away)
    parts = [
        call(
            functools.partial(field_without_inflow, other),
            [(VMEM, (elements, depth, half), f32)],
            core, *c, *bsn, *held(source),
            scratch=[VMEM((2 * WIDE, half), f32)],
            us=0 if other == 0 else 0,
            after=[out],
        )[0]
        for other, source in enumerate((halos, (got[0], got[1])))
    ]
    keep, send = call(
        inflow_of_cores,
        [(VMEM, (WIDE, half), f32)] * 2,
        core, *held((lead, resp, *chips, *steps)),
        us=20,
    )
    (field,) = call(
        whole_field,
        [(HBM, rhs.shape, f32)],
        core, *held((*parts, keep, swap(send))), *bu,
        scratch=[
            VMEM((WIDE, columns), f32),
            VMEM((elements, unknowns, columns), f32),
            dma((elements,)),
        ],
        us=1,
    )
    return by_row(field)


def solution(mesh):
    spec = P("sweep", "span", None, None)
    return jax.shard_map(
        per_device, mesh=mesh, in_specs=(spec,) * 6, out_specs=spec, check_vma=False
    )
```

```python
import functools

import jax
import jax.numpy as jnp
from jax import lax
from jax.experimental import pallas as pl
from jax.experimental.pallas import tpu as pltpu
from jax.sharding import PartitionSpec as P

VARS = 5
NODE = 5
FACE = VARS * NODE**2
WIDE = 128
SWEEPS = 2
CORES = 2
EARLY = (3, 1, 2)
LATE = (0,)
LIMIT = 24 * 1024 * 1024
MOST = 60 * 1024 * 1024
ANY = pl.ANY
HBM = pltpu.HBM
VMEM = pltpu.VMEM
SMEM = pltpu.SMEM


def face_runs(kind):
    if kind == "down":
        return [(var * NODE**3 + (NODE - 1) * NODE**2, NODE**2) for var in range(VARS)]
    b = NODE - 1 if kind == "high" else 0
    return [
        (var * NODE**3 + a * NODE**2 + b * NODE, NODE)
        for var in range(VARS)
        for a in range(NODE)
    ]


def split(x):
    top = x.astype(jnp.bfloat16)
    return top, (x - top.astype(jnp.float32)).astype(jnp.bfloat16)


def left(x):
    high, low = split(x)
    return jnp.concatenate([high, high, low], axis=1)


def right(x):
    high, low = split(x)
    return jnp.concatenate([high, low, high], axis=0)


def stacked(a, b):
    return jnp.dot(a, b, preferred_element_type=jnp.float32)


def padded(x, rows):
    short = rows - x.shape[0]
    return jnp.concatenate([x, jnp.zeros((short, x.shape[1]), x.dtype)], axis=0) if short else x


def call(kernel, outs, *args, scratch=(), us=1, after=(), limit=LIMIT, aliases=None):
    args = list(args) + [(ANY, x) for x in after]

    def body(*refs):
        given = len(args) - len(after)
        kernel(*refs[:given], *refs[len(args) :])

    return pl.pallas_call(
        body,
        out_shape=[jax.ShapeDtypeStruct(shape, kind) for _, shape, kind in outs],
        in_specs=[pl.BlockSpec(memory_space=space) for space, _ in args],
        out_specs=[pl.BlockSpec(memory_space=space) for space, _, _ in outs],
        scratch_shapes=list(scratch),
        input_output_aliases=aliases or {},
        compiler_params=pltpu.CompilerParams(vmem_limit_bytes=limit),
        cost_estimate=pl.CostEstimate(flops=int(us * 10**9), bytes_accessed=0, transcendentals=0),
        name=getattr(kernel, "func", kernel).__name__,
    )(*[array for _, array in args])


def start_faces(core_ref, field_ref, *refs):
    outs, sems = refs[:-1], refs[-1]
    half = outs[0].shape[-1]
    parts = []
    for k, out in enumerate(outs):
        own = core_ref[0] if k < 2 else 1 - core_ref[0]
        low = core_ref[2] if k % 2 == 0 else 1 - core_ref[2]
        part = pltpu.make_async_copy(
            field_ref.at[
                :, :, pl.ds((1 - low) * (NODE - 1) * NODE, NODE), :,
                pl.ds(pl.multiple_of(own * half, half), half),
            ],
            out,
            sems.at[k],
        )
        part.start()
        parts.append(part)
    for part in parts:
        part.wait()


def load_rows(pairs, sems):
    copies = []
    for k, (source, held) in enumerate(pairs):
        copies.append(pltpu.make_async_copy(source, held, sems.at[k]))
        copies[-1].start()
    return copies


def load_blocks(inv_ref, rhs_ref, up_ref, south_ref, north_ref, inv, rhs, blocks, sems):
    return [
        load_rows(
            [
                (inv_ref.at[e, :, 0, :], inv.at[e]),
                (rhs_ref.at[e, :, 0, :], rhs.at[e]),
                (south_ref.at[e, :, 0, :], blocks.at[e, 0]),
                (north_ref.at[e, :, 0, :], blocks.at[e, 1]),
                (up_ref.at[e, :, 0, :], blocks.at[e, 2]),
            ],
            sems.at[e],
        )
        for e in range(inv_ref.shape[0])
    ]


def fill_columns(e, depth, rhs, blocks, columns):
    wide = rhs.shape[2]
    columns[:, :wide] = right(padded(rhs[e], depth))
    for k in range(3):
        at = wide + k * WIDE
        block = right(padded(blocks[e, k], depth))
        columns[:, at : at + FACE] = block


def fold_faces(inv_ref, rhs_ref, up_ref, south_ref, north_ref, faces_ref,
               inv, rhs, blocks, rows, columns, sems):
    elements, depth, wide = inv.shape[0], rows.shape[1], rhs.shape[2]
    half = wide // CORES
    copies = load_blocks(inv_ref, rhs_ref, up_ref, south_ref, north_ref, inv, rhs, blocks, sems)
    rows[...] = jnp.zeros_like(rows)
    columns[...] = jnp.zeros_like(columns)
    for e in range(elements):
        copies[e][0].wait()
        for f, kind in enumerate(("down", "high", "low")):
            at = f * WIDE
            for first, length in face_runs(kind):
                rows[at : at + length, : inv.shape[2]] = inv[e, first : first + length, :]
                at += length
        for copy in copies[e][1:]:
            copy.wait()
        fill_columns(e, depth, rhs, blocks, columns)
        product = stacked(left(rows[...]), columns[...])
        for k in range(CORES):
            faces_ref[k, e, :, :half] = product[:, k * half : (k + 1) * half]
            faces_ref[k, e, :, half:] = product[:, wide:]


def fold_element(e, raw, outs, inv, rhs, blocks, rows, columns, sems):
    inv_ref, rhs_ref, up_ref, south_ref, north_ref = raw
    unknowns = inv.shape[1]
    depth, wide = rows.shape[1], rhs.shape[2]
    copies = load_rows(
        [
            (inv_ref.at[e, :, 0, :], inv.at[0]),
            (rhs_ref.at[e, :, 0, :], rhs.at[0]),
            (south_ref.at[e, :, 0, :], blocks.at[0, 0]),
            (north_ref.at[e, :, 0, :], blocks.at[0, 1]),
            (up_ref.at[e, :, 0, :], blocks.at[0, 2]),
        ],
        sems,
    )
    rows[...] = jnp.zeros_like(rows)
    columns[...] = jnp.zeros_like(columns)
    for copy in copies:
        copy.wait()
    rows[:unknowns, :unknowns] = inv[0]
    fill_columns(0, depth, rhs, blocks, columns)
    product = stacked(left(rows[...]), columns[...])
    c_ref, bsn_ref, bu_ref = outs
    c_ref[...] = product[:, :wide]
    bsn_ref[...] = left(product[:, wide : wide + 2 * WIDE])
    bu_ref[...] = left(product[:, wide + 2 * WIDE :])


def fold_rest(core_ref, *refs):
    raw, scratch = refs[:5], refs[-6:]
    outs = refs[5:-6]
    for e in range(len(outs) // 3 - 1, -1, -1):
        one = functools.partial(fold_element, e, raw, outs[3 * e : 3 * e + 3], *scratch)
        if e:
            one()
        else:
            pl.when(core_ref[0] == 1)(one)


def chip_blocks(faces_ref, fc_ref, fsn_ref, fu_ref, resp_ref, step_ref, const_ref, high_ref, low_ref, held):
    elements, half = faces_ref.shape[1], fc_ref.shape[2]
    count = CORES * elements
    for e in range(count):
        source = faces_ref.at[e // elements, e % elements]
        fc_ref[e] = source[:, :half]
        fsn_ref[e] = left(source[:, half : half + 2 * WIDE])
        own = source[:, half + 2 * WIDE :]
        fu_ref[e] = left(own)
        held[...] = -stacked(fu_ref[e], right(held[:WIDE, :])) if e else -own
        resp_ref[e] = left(held[...])
    step_ref[...] = held[:WIDE, :]
    high_ref[WIDE:, elements * 2 * WIDE :] = jnp.zeros_like(high_ref[WIDE:, elements * 2 * WIDE :])
    low_ref[WIDE:, elements * 2 * WIDE :] = jnp.zeros_like(low_ref[WIDE:, elements * 2 * WIDE :])
    for rows, last in ((slice(0, WIDE), count - 1), (slice(WIDE, 2 * WIDE), elements - 1)):
        passed = None
        for e in range(last, -1, -1):
            source = faces_ref.at[e // elements, e % elements]
            block = source[:WIDE, :]
            value = block if passed is None else stacked(left(passed), right(block))
            const = value[:, :half] if passed is None else const + value[:, :half]
            at = slice(e * 2 * WIDE, (e + 1) * 2 * WIDE)
            high_ref[rows, at], low_ref[rows, at] = split(value[:, half : half + 2 * WIDE])
            passed = -value[:, half + 2 * WIDE :]
        const_ref[rows, :] = const


def south_north(core_ref, k):
    return pl.multiple_of(((1 - core_ref[2]) if k == 0 else core_ref[2]) * WIDE, WIDE)


def traces(const, high, low, halo_high, halo_low):
    dot = functools.partial(jnp.dot, preferred_element_type=jnp.float32)
    return const - (dot(high, halo_high) + (dot(high, halo_low) + dot(low, halo_high)))


def take_halos(kinds, core_ref, halos, halo_high, halo_low, held, sems):
    elements = held.shape[1]
    copies = load_rows([(halo.at[:, :, 0, :], held.at[k]) for k, halo in enumerate(halos)], sems)
    for k, kind in enumerate(kinds):
        copies[k].wait()
        owner = core_ref[0] if kind < 2 else 1 - core_ref[0]
        for e in range(elements):
            row = 2 * WIDE * (owner * elements + e) + south_north(core_ref, kind % 2)
            at = pl.ds(pl.multiple_of(row, WIDE), WIDE)
            halo_high[at, :], halo_low[at, :] = split(padded(held[k, e], WIDE))


def early_halos(core_ref, *refs):
    take_halos(EARLY, core_ref, refs[: len(EARLY)], *refs[len(EARLY) :])


def first_traces(core_ref, const_ref, high_ref, low_ref, *refs):
    count = len(LATE)
    halos, raw, refs = refs[:count], refs[count : count + 5], refs[count + 7 :]
    halo_high, halo_low, out_ref, *outs = refs[:6]
    held, sems, *scratch = refs[6:]
    take_halos(LATE, core_ref, halos, halo_high, halo_low, held, sems)
    out_ref[...] = traces(
        const_ref[:WIDE, :], high_ref[:WIDE, :], low_ref[:WIDE, :], halo_high[...], halo_low[...]
    )
    pl.when(core_ref[0] == 0)(functools.partial(fold_element, 0, raw, outs, *scratch))


def other_faces(fc_ref, fsn_ref, fu_ref, halo_high, halo_low, faces_ref):
    trace = None
    for e in range(fc_ref.shape[0]):
        at = slice(2 * e * WIDE, 2 * (e + 1) * WIDE)
        high = halo_high[at, :]
        faces = fc_ref[e] - stacked(fsn_ref[e], jnp.concatenate([high, halo_low[at, :], high], axis=0))
        if e:
            faces = faces - stacked(fu_ref[e], right(trace))
        trace = faces[:WIDE]
        faces_ref[e] = faces[WIDE:]


def last_traces(core_ref, const_ref, high_ref, low_ref, second_ref, first_ref, out_ref, lead_ref, away_ref,
                halo_high, halo_low):
    count = first_ref.shape[0]
    elements = count // CORES
    for e in range(count):
        for k, ref in enumerate((first_ref, second_ref)):
            at = pl.ds(pl.multiple_of(south_north(core_ref, k) + 2 * e * WIDE, WIDE), WIDE)
            halo_high[at, :], halo_low[at, :] = split(ref[e])
    both = traces(const_ref[...], high_ref[...], low_ref[...], halo_high[...], halo_low[...])
    out_ref[...] = both[:WIDE]
    lead_ref[...] = both[WIDE:]
    other = (1 - core_ref[0]) * elements
    for e in range(elements):
        away_ref[0, e] = first_ref[other + e]
        away_ref[1, e] = second_ref[other + e]


def through_chips(core_ref, inflow_ref, chips, steps):
    inflow_ref[...] = jnp.zeros_like(inflow_ref)
    for back in range(len(chips), 0, -1):

        @pl.when(core_ref[1] >= back)
        def _():
            if back == len(chips):
                inflow_ref[...] = chips[back - 1][...]
            else:
                passed = stacked(left(steps[back - 1][...]), right(inflow_ref[...]))
                inflow_ref[...] = chips[back - 1][...] + passed


def next_faces(core_ref, faces_ref, resp_ref, *refs):
    first_ref, second_ref, inflow_ref, both = refs[-4:]
    count = (len(refs) - 3) // 2
    through_chips(core_ref, inflow_ref, refs[:count], refs[count:-4])
    inflow = right(inflow_ref[...])
    first = pl.multiple_of(core_ref[2] * WIDE, WIDE)
    second = pl.multiple_of((1 - core_ref[2]) * WIDE, WIDE)
    for e in range(faces_ref.shape[0]):
        both[e] = faces_ref[e] + stacked(resp_ref[e, WIDE:, :], inflow)
    for e in range(faces_ref.shape[0]):
        first_ref[e] = both[e, pl.ds(first, WIDE), :]
        second_ref[e] = both[e, pl.ds(second, WIDE), :]


def inflow_of_cores(core_ref, lead_ref, resp_ref, *refs):
    keep_ref, send_ref = refs[-2:]
    count = (len(refs) - 1) // 2
    through_chips(core_ref, keep_ref, refs[:count], refs[count:-2])
    last = resp_ref.shape[0] // CORES - 1

    @pl.when(core_ref[0] == 0)
    def _():
        send_ref[...] = lead_ref[...] + stacked(resp_ref[last, :WIDE, :], right(keep_ref[...]))

    @pl.when(core_ref[0] == 1)
    def _():
        send_ref[...] = keep_ref[...]
        keep_ref[...] = lead_ref[...] + stacked(resp_ref[last, :WIDE, :], right(send_ref[...]))


def join(core_ref, keep_ref, got_ref, inflow_ref):
    half = keep_ref.shape[1]

    @pl.when(core_ref[0] == 0)
    def _():
        inflow_ref[:, :half] = keep_ref[...]
        inflow_ref[:, half:] = got_ref[...]

    @pl.when(core_ref[0] == 1)
    def _():
        inflow_ref[:, :half] = got_ref[...]
        inflow_ref[:, half:] = keep_ref[...]


def field_without_inflow(other, core_ref, *refs):
    first_ref, second_ref, p_ref, halo = refs[-4:]
    elements, half = p_ref.shape[0], p_ref.shape[2]
    c_refs, bsn_refs = refs[: elements + 1], refs[elements + 1 : 2 * elements + 2]
    own = 0 if other else core_ref[0] * elements
    at = pl.ds(pl.multiple_of((1 - core_ref[0] if other else core_ref[0]) * half, half), half)
    for e in range(elements):
        for k, ref in enumerate((first_ref, second_ref)):
            halo[pl.ds(south_north(core_ref, k), WIDE), :] = ref[own + e]
        halos = right(halo[...])

        def place(c_ref, bsn_ref):
            p_ref[e] = c_ref[:, at] - stacked(bsn_ref[...], halos)

        by_core(core_ref, e, place, c_refs, bsn_refs)


def by_core(core_ref, e, use, *stacks):
    if e:
        use(*[refs[e + 1] for refs in stacks])
    else:
        for k in range(CORES):
            pl.when(core_ref[0] == k)(functools.partial(use, *[refs[k] for refs in stacks]))


def whole_field(core_ref, own_ref, other_ref, keep_ref, got_ref, *refs):
    bu_refs, (out_ref, inflow_ref, held, sems) = refs[:-4], refs[-4:]
    join(core_ref, keep_ref, got_ref, inflow_ref)
    elements, unknowns = held.shape[:2]
    half = keep_ref.shape[1]
    copies = []
    for e in range(elements):
        if e:
            at = 0
            for first, length in face_runs("down"):
                inflow_ref[at : at + length, :] = held[e - 1, first : first + length, :]
                at += length
        inflow = right(inflow_ref[...])

        def place(own, bu_ref):
            change = stacked(bu_ref[...], inflow)[:unknowns]
            for k in range(CORES):
                part = own_ref if k == own else other_ref
                at = slice(k * half, (k + 1) * half)
                held[e, :, at] = part[e, :unknowns, :] - change[:, at]

        for k in range(CORES):
            pl.when(core_ref[0] == k)(functools.partial(place, k, bu_refs[e + 1 if e else k]))
        copy = pltpu.make_async_copy(held.at[e], out_ref.at[e, :, 0, :], sems.at[e])
        copy.start()
        copies.append(copy)
    for copy in copies:
        copy.wait()


def ring(axis, by):
    count = lax.axis_size(axis)
    return [(i, (i + by) % count) for i in range(count)]


def per_device(right_side, start_field, block_inverse, upwind_block, south_block, north_block):
    by_row = lambda x: x.transpose(0, 2, 1, 3)
    rhs, start, inverse, upwind, south, north = map(
        by_row, (right_side, start_field, block_inverse, upwind_block, south_block, north_block)
    )
    elements, unknowns, _, columns = rhs.shape
    depth = -(-unknowns // 128) * 128
    half = columns // CORES
    count = CORES * elements
    devices, spans = lax.axis_size("sweep"), lax.axis_size("span")
    place = lax.axis_index("sweep")
    odd = lax.axis_index("span") % 2
    where = jnp.stack([place % CORES, place // CORES, odd]).astype(jnp.int32)
    dma = pltpu.SemaphoreType.DMA
    f32, bf16 = jnp.float32, jnp.bfloat16
    core = (SMEM, where)
    face = (elements, FACE, 1, half)

    def held(arrays):
        return [(VMEM, x) for x in arrays]

    def swap(x):
        return lax.ppermute(x, "sweep", [(i, i ^ 1) for i in range(devices)])

    def from_chips(x):
        return [
            lax.ppermute(x, "sweep", ring("sweep", CORES * back))
            for back in range(1, devices // CORES)
        ]

    def along_span(x, second, other_core):
        pairs = []
        for i in range(devices):
            for j in range(spans):
                by = 1 if (j + second) % 2 == 0 else -1
                pairs.append((i * spans + j, (i ^ other_core) * spans + (j + by) % spans))
        return lax.ppermute(x, ("sweep", "span"), pairs)

    runs = start.reshape(elements, NODE**2, VARS * NODE, 1, columns)
    found = call(
        start_faces,
        [(VMEM, (elements, NODE**2, NODE, 1, half), f32)] * 4,
        core, (HBM, runs),
        scratch=[dma((4,))],
    )
    halos = [along_span(found[k].reshape(face), k % 2, k // 2) for k in range(4)]
    raw = [(HBM, x) for x in (inverse, rhs, upwind, south, north)]
    raw_scratch = [
        VMEM((elements, unknowns, unknowns), f32),
        VMEM((elements, unknowns, columns), f32),
        VMEM((elements, 3, unknowns, FACE), f32),
    ]
    fold_scratch = [VMEM((3 * depth, columns + 3 * WIDE), bf16), dma((elements, 5))]
    (own,) = call(
        fold_faces,
        [(VMEM, (CORES, elements, 3 * WIDE, half + 3 * WIDE), f32)],
        *raw,
        scratch=raw_scratch + [VMEM((3 * WIDE, depth), f32)] + fold_scratch,
        us=0,
        limit=MOST,
        after=found,
    )
    cores = lax.all_to_all(
        own, "sweep", 0, 0, axis_index_groups=[[i, i + 1] for i in range(0, devices, CORES)]
    )
    fc, fsn, fu, resp, step, *trace_blocks = call(
        chip_blocks,
        [
            (VMEM, (count, 3 * WIDE, half), f32),
            (VMEM, (count, 3 * WIDE, 6 * WIDE), bf16),
            (VMEM, (count, 3 * WIDE, 3 * WIDE), bf16),
            (VMEM, (count, 3 * WIDE, 3 * WIDE), bf16),
            (VMEM, (WIDE, WIDE), f32),
            (VMEM, (2 * WIDE, half), f32),
        ]
        + [(VMEM, (2 * WIDE, 2 * count * WIDE), bf16)] * 2,
        (VMEM, cores),
        scratch=[VMEM((3 * WIDE, WIDE), f32)],
        us=0,
    )
    steps = from_chips(step)[:-1]
    halo_split = (2 * count * WIDE, half)
    folded = [
        (VMEM, (depth, columns), f32),
        (VMEM, (depth, 6 * WIDE), bf16),
        (VMEM, (depth, 3 * WIDE), bf16),
    ]
    one_scratch = [VMEM((1,) + x.shape[1:], f32) for x in raw_scratch]
    one_scratch += [VMEM((depth, depth), f32), VMEM((3 * depth, columns + 3 * WIDE), bf16), dma((5,))]
    halo_parts = call(
        early_halos,
        [(VMEM, halo_split, bf16)] * 2,
        core, *[(HBM, halos[k]) for k in EARLY],
        scratch=[VMEM((len(EARLY), elements, FACE, half), f32), dma((len(EARLY),))],
        us=1,
    )
    folded_early = call(
        first_traces,
        [(VMEM, halo_split, bf16)] * 2 + [(VMEM, (WIDE, half), f32)] + folded,
        core, *held(trace_blocks), *[(HBM, halos[k]) for k in LATE], *raw, *held(halo_parts),
        scratch=[VMEM((len(LATE), elements, FACE, half), f32), dma((len(LATE),))] + one_scratch,
        us=2,
        aliases={9 + len(LATE): 0, 10 + len(LATE): 1},
    )
    halo_parts, out, early = folded_early[:2], folded_early[2], folded_early[3:]
    chips = from_chips(out)
    (faces,) = call(
        other_faces,
        [(VMEM, (count, 2 * WIDE, half), f32)],
        *held((fc, fsn, fu, *halo_parts)),
        us=2,
        after=steps,
    )
    last = call(
        next_faces,
        [(VMEM, (count, WIDE, half), f32)] * 2,
        core, *held((faces, resp, *chips, *steps)),
        scratch=[VMEM((WIDE, half), f32), VMEM((count, 2 * WIDE, half), f32)],
        us=1,
    )
    halos = [along_span(last[k], k, 0) for k in (1, 0)][::-1]
    late = call(
        fold_rest,
        folded * elements,
        core, *raw,
        scratch=one_scratch,
        us=10,
        after=last,
    )
    c, bsn, bu = [held([early[k], *late[k::3]]) for k in range(3)]
    out, lead, away = call(
        last_traces,
        [
            (VMEM, (WIDE, half), f32),
            (VMEM, (WIDE, half), f32),
            (VMEM, (2, elements, WIDE, half), f32),
        ],
        core, *held((*trace_blocks, *halos[::-1])),
        scratch=[VMEM(halo_split, bf16)] * 2,
        us=1,
        after=late[:1],
    )
    chips = from_chips(out)
    got = swap(away)
    parts = [
        call(
            functools.partial(field_without_inflow, other),
            [(VMEM, (elements, depth, half), f32)],
            core, *c, *bsn, *held(source),
            scratch=[VMEM((2 * WIDE, half), f32)],
            us=0 if other == 0 else 0,
            after=[out],
        )[0]
        for other, source in enumerate((halos, (got[0], got[1])))
    ]
    keep, send = call(
        inflow_of_cores,
        [(VMEM, (WIDE, half), f32)] * 2,
        core, *held((lead, resp, *chips, *steps)),
        us=20,
    )
    (field,) = call(
        whole_field,
        [(HBM, rhs.shape, f32)],
        core, *held((*parts, keep, swap(send))), *bu,
        scratch=[
            VMEM((WIDE, columns), f32),
            VMEM((elements, unknowns, columns), f32),
            dma((elements,)),
        ],
        us=1,
    )
    return by_row(field)


def solution(mesh):
    spec = P("sweep", "span", None, None)
    return jax.shard_map(
        per_device, mesh=mesh, in_specs=(spec,) * 6, out_specs=spec, check_vma=False
    )
```

```python
import functools

import jax
import jax.numpy as jnp
from jax import lax
from jax.experimental import pallas as pl
from jax.experimental.pallas import tpu as pltpu
from jax.sharding import PartitionSpec as P

VARS = 5
NODE = 5
FACE = VARS * NODE**2
WIDE = 128
SWEEPS = 2
CORES = 2
EARLY = (0, 1, 3)
LATE = (2,)
LIMIT = 24 * 1024 * 1024
MOST = 60 * 1024 * 1024
ANY = pl.ANY
HBM = pltpu.HBM
VMEM = pltpu.VMEM
SMEM = pltpu.SMEM


def face_runs(kind):
    if kind == "down":
        return [(var * NODE**3 + (NODE - 1) * NODE**2, NODE**2) for var in range(VARS)]
    b = NODE - 1 if kind == "high" else 0
    return [
        (var * NODE**3 + a * NODE**2 + b * NODE, NODE)
        for var in range(VARS)
        for a in range(NODE)
    ]


def split(x):
    top = x.astype(jnp.bfloat16)
    return top, (x - top.astype(jnp.float32)).astype(jnp.bfloat16)


def left(x):
    high, low = split(x)
    return jnp.concatenate([high, high, low], axis=1)


def right(x):
    high, low = split(x)
    return jnp.concatenate([high, low, high], axis=0)


def stacked(a, b):
    return jnp.dot(a, b, preferred_element_type=jnp.float32)


def padded(x, rows):
    short = rows - x.shape[0]
    return jnp.concatenate([x, jnp.zeros((short, x.shape[1]), x.dtype)], axis=0) if short else x


def call(kernel, outs, *args, scratch=(), us=1, after=(), limit=LIMIT, aliases=None):
    args = list(args) + [(ANY, x) for x in after]

    def body(*refs):
        given = len(args) - len(after)
        kernel(*refs[:given], *refs[len(args) :])

    return pl.pallas_call(
        body,
        out_shape=[jax.ShapeDtypeStruct(shape, kind) for _, shape, kind in outs],
        in_specs=[pl.BlockSpec(memory_space=space) for space, _ in args],
        out_specs=[pl.BlockSpec(memory_space=space) for space, _, _ in outs],
        scratch_shapes=list(scratch),
        input_output_aliases=aliases or {},
        compiler_params=pltpu.CompilerParams(vmem_limit_bytes=limit),
        cost_estimate=pl.CostEstimate(flops=int(us * 10**9), bytes_accessed=0, transcendentals=0),
        name=getattr(kernel, "func", kernel).__name__,
    )(*[array for _, array in args])


def start_faces(core_ref, field_ref, *refs):
    outs, sems = refs[:-1], refs[-1]
    half = outs[0].shape[-1]
    parts = []
    for k, out in enumerate(outs):
        own = core_ref[0] if k < 2 else 1 - core_ref[0]
        low = core_ref[2] if k % 2 == 0 else 1 - core_ref[2]
        part = pltpu.make_async_copy(
            field_ref.at[
                :, :, pl.ds((1 - low) * (NODE - 1) * NODE, NODE), :,
                pl.ds(pl.multiple_of(own * half, half), half),
            ],
            out,
            sems.at[k],
        )
        part.start()
        parts.append(part)
    for part in parts:
        part.wait()


def load_rows(pairs, sems):
    copies = []
    for k, (source, held) in enumerate(pairs):
        copies.append(pltpu.make_async_copy(source, held, sems.at[k]))
        copies[-1].start()
    return copies


def load_blocks(inv_ref, rhs_ref, up_ref, south_ref, north_ref, inv, rhs, blocks, sems):
    return [
        load_rows(
            [
                (inv_ref.at[e, :, 0, :], inv.at[e]),
                (rhs_ref.at[e, :, 0, :], rhs.at[e]),
                (south_ref.at[e, :, 0, :], blocks.at[e, 0]),
                (north_ref.at[e, :, 0, :], blocks.at[e, 1]),
                (up_ref.at[e, :, 0, :], blocks.at[e, 2]),
            ],
            sems.at[e],
        )
        for e in range(inv_ref.shape[0])
    ]


def fill_columns(e, depth, rhs, blocks, columns):
    wide = rhs.shape[2]
    columns[:, :wide] = right(padded(rhs[e], depth))
    for k in range(3):
        at = wide + k * WIDE
        block = right(padded(blocks[e, k], depth))
        columns[:, at : at + FACE] = block


def fold_faces(inv_ref, rhs_ref, up_ref, south_ref, north_ref, faces_ref,
               inv, rhs, blocks, rows, columns, sems):
    elements, depth, wide = inv.shape[0], rows.shape[1], rhs.shape[2]
    half = wide // CORES
    copies = load_blocks(inv_ref, rhs_ref, up_ref, south_ref, north_ref, inv, rhs, blocks, sems)
    rows[...] = jnp.zeros_like(rows)
    columns[...] = jnp.zeros_like(columns)
    for e in range(elements):
        copies[e][0].wait()
        for f, kind in enumerate(("down", "high", "low")):
            at = f * WIDE
            for first, length in face_runs(kind):
                rows[at : at + length, : inv.shape[2]] = inv[e, first : first + length, :]
                at += length
        for copy in copies[e][1:]:
            copy.wait()
        fill_columns(e, depth, rhs, blocks, columns)
        product = stacked(left(rows[...]), columns[...])
        for k in range(CORES):
            faces_ref[k, e, :, :half] = product[:, k * half : (k + 1) * half]
            faces_ref[k, e, :, half:] = product[:, wide:]


def fold_element(e, raw, outs, inv, rhs, blocks, rows, columns, sems):
    inv_ref, rhs_ref, up_ref, south_ref, north_ref = raw
    unknowns = inv.shape[1]
    depth, wide = rows.shape[1], rhs.shape[2]
    copies = load_rows(
        [
            (inv_ref.at[e, :, 0, :], inv.at[0]),
            (rhs_ref.at[e, :, 0, :], rhs.at[0]),
            (south_ref.at[e, :, 0, :], blocks.at[0, 0]),
            (north_ref.at[e, :, 0, :], blocks.at[0, 1]),
            (up_ref.at[e, :, 0, :], blocks.at[0, 2]),
        ],
        sems,
    )
    rows[...] = jnp.zeros_like(rows)
    columns[...] = jnp.zeros_like(columns)
    for copy in copies:
        copy.wait()
    rows[:unknowns, :unknowns] = inv[0]
    fill_columns(0, depth, rhs, blocks, columns)
    product = stacked(left(rows[...]), columns[...])
    c_ref, bsn_ref, bu_ref = outs
    c_ref[...] = product[:, :wide]
    bsn_ref[...] = left(product[:, wide : wide + 2 * WIDE])
    bu_ref[...] = left(product[:, wide + 2 * WIDE :])


def fold_rest(core_ref, *refs):
    raw, scratch = refs[:5], refs[-6:]
    outs = refs[5:-6]
    for e in range(len(outs) // 3 - 1, -1, -1):
        one = functools.partial(fold_element, e, raw, outs[3 * e : 3 * e + 3], *scratch)
        if e:
            one()
        else:
            pl.when(core_ref[0] == 1)(one)


def chip_blocks(faces_ref, fc_ref, fsn_ref, fu_ref, resp_ref, step_ref, const_ref, high_ref, low_ref, held):
    elements, half = faces_ref.shape[1], fc_ref.shape[2]
    count = CORES * elements
    for e in range(count):
        source = faces_ref.at[e // elements, e % elements]
        fc_ref[e] = source[:, :half]
        fsn_ref[e] = left(source[:, half : half + 2 * WIDE])
        own = source[:, half + 2 * WIDE :]
        fu_ref[e] = left(own)
        held[...] = -stacked(fu_ref[e], right(held[:WIDE, :])) if e else -own
        resp_ref[e] = left(held[...])
    step_ref[...] = held[:WIDE, :]
    high_ref[WIDE:, elements * 2 * WIDE :] = jnp.zeros_like(high_ref[WIDE:, elements * 2 * WIDE :])
    low_ref[WIDE:, elements * 2 * WIDE :] = jnp.zeros_like(low_ref[WIDE:, elements * 2 * WIDE :])
    for rows, last in ((slice(0, WIDE), count - 1), (slice(WIDE, 2 * WIDE), elements - 1)):
        passed = None
        for e in range(last, -1, -1):
            source = faces_ref.at[e // elements, e % elements]
            block = source[:WIDE, :]
            value = block if passed is None else stacked(left(passed), right(block))
            const = value[:, :half] if passed is None else const + value[:, :half]
            at = slice(e * 2 * WIDE, (e + 1) * 2 * WIDE)
            high_ref[rows, at], low_ref[rows, at] = split(value[:, half : half + 2 * WIDE])
            passed = -value[:, half + 2 * WIDE :]
        const_ref[rows, :] = const


def south_north(core_ref, k):
    return pl.multiple_of(((1 - core_ref[2]) if k == 0 else core_ref[2]) * WIDE, WIDE)


def traces(const, high, low, halo_high, halo_low):
    dot = functools.partial(jnp.dot, preferred_element_type=jnp.float32)
    return const - (dot(high, halo_high) + (dot(high, halo_low) + dot(low, halo_high)))


def take_halos(kinds, core_ref, halos, halo_high, halo_low, held, sems):
    elements = held.shape[1]
    copies = load_rows([(halo.at[:, :, 0, :], held.at[k]) for k, halo in enumerate(halos)], sems)
    for k, kind in enumerate(kinds):
        copies[k].wait()
        owner = core_ref[0] if kind < 2 else 1 - core_ref[0]
        for e in range(elements):
            row = 2 * WIDE * (owner * elements + e) + south_north(core_ref, kind % 2)
            at = pl.ds(pl.multiple_of(row, WIDE), WIDE)
            halo_high[at, :], halo_low[at, :] = split(padded(held[k, e], WIDE))


def early_halos(core_ref, *refs):
    take_halos(EARLY, core_ref, refs[: len(EARLY)], *refs[len(EARLY) :])


def first_traces(core_ref, const_ref, high_ref, low_ref, *refs):
    count = len(LATE)
    halos, raw, refs = refs[:count], refs[count : count + 5], refs[count + 7 :]
    halo_high, halo_low, out_ref, *outs = refs[:6]
    held, sems, *scratch = refs[6:]
    take_halos(LATE, core_ref, halos, halo_high, halo_low, held, sems)
    out_ref[...] = traces(
        const_ref[:WIDE, :], high_ref[:WIDE, :], low_ref[:WIDE, :], halo_high[...], halo_low[...]
    )
    pl.when(core_ref[0] == 0)(functools.partial(fold_element, 0, raw, outs, *scratch))


def other_faces(fc_ref, fsn_ref, fu_ref, halo_high, halo_low, faces_ref):
    trace = None
    for e in range(fc_ref.shape[0]):
        at = slice(2 * e * WIDE, 2 * (e + 1) * WIDE)
        high = halo_high[at, :]
        faces = fc_ref[e] - stacked(fsn_ref[e], jnp.concatenate([high, halo_low[at, :], high], axis=0))
        if e:
            faces = faces - stacked(fu_ref[e], right(trace))
        trace = faces[:WIDE]
        faces_ref[e] = faces[WIDE:]


def last_traces(rows, core_ref, const_ref, high_ref, low_ref, second_ref, first_ref, out_ref, *refs):
    halo_high, halo_low = refs[-2:]
    count = first_ref.shape[0]
    for e in range(count):
        for k, ref in enumerate((first_ref, second_ref)):
            at = pl.ds(pl.multiple_of(south_north(core_ref, k) + 2 * e * WIDE, WIDE), WIDE)
            halo_high[at, :], halo_low[at, :] = split(ref[e])
    out_ref[...] = traces(
        const_ref[rows, :], high_ref[rows, :], low_ref[rows, :], halo_high[...], halo_low[...]
    )
    if len(refs) > 2:
        elements = count // CORES
        other = (1 - core_ref[0]) * elements
        for e in range(elements):
            refs[0][0, e] = first_ref[other + e]
            refs[0][1, e] = second_ref[other + e]


def through_chips(core_ref, inflow_ref, chips, steps):
    inflow_ref[...] = jnp.zeros_like(inflow_ref)
    for back in range(len(chips), 0, -1):

        @pl.when(core_ref[1] >= back)
        def _():
            if back == len(chips):
                inflow_ref[...] = chips[back - 1][...]
            else:
                passed = stacked(left(steps[back - 1][...]), right(inflow_ref[...]))
                inflow_ref[...] = chips[back - 1][...] + passed


def next_faces(core_ref, faces_ref, resp_ref, *refs):
    first_ref, second_ref, inflow_ref, both = refs[-4:]
    count = (len(refs) - 3) // 2
    through_chips(core_ref, inflow_ref, refs[:count], refs[count:-4])
    inflow = right(inflow_ref[...])
    first = pl.multiple_of(core_ref[2] * WIDE, WIDE)
    second = pl.multiple_of((1 - core_ref[2]) * WIDE, WIDE)
    for e in range(faces_ref.shape[0]):
        both[e] = faces_ref[e] + stacked(resp_ref[e, WIDE:, :], inflow)
    for e in range(faces_ref.shape[0]):
        first_ref[e] = both[e, pl.ds(first, WIDE), :]
        second_ref[e] = both[e, pl.ds(second, WIDE), :]


def inflow_of_cores(core_ref, lead_ref, resp_ref, *refs):
    keep_ref, send_ref = refs[-2:]
    count = (len(refs) - 1) // 2
    through_chips(core_ref, keep_ref, refs[:count], refs[count:-2])
    last = resp_ref.shape[0] // CORES - 1

    @pl.when(core_ref[0] == 0)
    def _():
        send_ref[...] = lead_ref[...] + stacked(resp_ref[last, :WIDE, :], right(keep_ref[...]))

    @pl.when(core_ref[0] == 1)
    def _():
        send_ref[...] = keep_ref[...]
        keep_ref[...] = lead_ref[...] + stacked(resp_ref[last, :WIDE, :], right(send_ref[...]))


def join(core_ref, keep_ref, got_ref, inflow_ref):
    half = keep_ref.shape[1]

    @pl.when(core_ref[0] == 0)
    def _():
        inflow_ref[:, :half] = keep_ref[...]
        inflow_ref[:, half:] = got_ref[...]

    @pl.when(core_ref[0] == 1)
    def _():
        inflow_ref[:, :half] = got_ref[...]
        inflow_ref[:, half:] = keep_ref[...]


def field_without_inflow(other, core_ref, *refs):
    first_ref, second_ref, p_ref, halo = refs[-4:]
    elements, half = p_ref.shape[0], p_ref.shape[2]
    c_refs, bsn_refs = refs[: elements + 1], refs[elements + 1 : 2 * elements + 2]
    own = 0 if other else core_ref[0] * elements
    at = pl.ds(pl.multiple_of((1 - core_ref[0] if other else core_ref[0]) * half, half), half)
    for e in range(elements):
        for k, ref in enumerate((first_ref, second_ref)):
            halo[pl.ds(south_north(core_ref, k), WIDE), :] = ref[own + e]
        halos = right(halo[...])

        def place(c_ref, bsn_ref):
            p_ref[e] = c_ref[:, at] - stacked(bsn_ref[...], halos)

        by_core(core_ref, e, place, c_refs, bsn_refs)


def by_core(core_ref, e, use, *stacks):
    if e:
        use(*[refs[e + 1] for refs in stacks])
    else:
        for k in range(CORES):
            pl.when(core_ref[0] == k)(functools.partial(use, *[refs[k] for refs in stacks]))


def whole_field(core_ref, own_ref, other_ref, keep_ref, got_ref, *refs):
    bu_refs, (out_ref, inflow_ref, held, sems) = refs[:-4], refs[-4:]
    join(core_ref, keep_ref, got_ref, inflow_ref)
    elements, unknowns = held.shape[:2]
    half = keep_ref.shape[1]
    copies = []
    for e in range(elements):
        if e:
            at = 0
            for first, length in face_runs("down"):
                inflow_ref[at : at + length, :] = held[e - 1, first : first + length, :]
                at += length
        inflow = right(inflow_ref[...])

        def place(own, bu_ref):
            change = stacked(bu_ref[...], inflow)[:unknowns]
            for k in range(CORES):
                part = own_ref if k == own else other_ref
                at = slice(k * half, (k + 1) * half)
                held[e, :, at] = part[e, :unknowns, :] - change[:, at]

        for k in range(CORES):
            pl.when(core_ref[0] == k)(functools.partial(place, k, bu_refs[e + 1 if e else k]))
        copy = pltpu.make_async_copy(held.at[e], out_ref.at[e, :, 0, :], sems.at[e])
        copy.start()
        copies.append(copy)
    for copy in copies:
        copy.wait()


def ring(axis, by):
    count = lax.axis_size(axis)
    return [(i, (i + by) % count) for i in range(count)]


def per_device(right_side, start_field, block_inverse, upwind_block, south_block, north_block):
    by_row = lambda x: x.transpose(0, 2, 1, 3)
    rhs, start, inverse, upwind, south, north = map(
        by_row, (right_side, start_field, block_inverse, upwind_block, south_block, north_block)
    )
    elements, unknowns, _, columns = rhs.shape
    depth = -(-unknowns // 128) * 128
    half = columns // CORES
    count = CORES * elements
    devices, spans = lax.axis_size("sweep"), lax.axis_size("span")
    place = lax.axis_index("sweep")
    odd = lax.axis_index("span") % 2
    where = jnp.stack([place % CORES, place // CORES, odd]).astype(jnp.int32)
    dma = pltpu.SemaphoreType.DMA
    f32, bf16 = jnp.float32, jnp.bfloat16
    core = (SMEM, where)
    face = (elements, FACE, 1, half)

    def held(arrays):
        return [(VMEM, x) for x in arrays]

    def swap(x):
        return lax.ppermute(x, "sweep", [(i, i ^ 1) for i in range(devices)])

    def from_chips(x):
        return [
            lax.ppermute(x, "sweep", ring("sweep", CORES * back))
            for back in range(1, devices // CORES)
        ]

    def along_span(x, second, other_core):
        pairs = []
        for i in range(devices):
            for j in range(spans):
                by = 1 if (j + second) % 2 == 0 else -1
                pairs.append((i * spans + j, (i ^ other_core) * spans + (j + by) % spans))
        return lax.ppermute(x, ("sweep", "span"), pairs)

    runs = start.reshape(elements, NODE**2, VARS * NODE, 1, columns)
    found = call(
        start_faces,
        [(VMEM, (elements, NODE**2, NODE, 1, half), f32)] * 4,
        core, (HBM, runs),
        scratch=[dma((4,))],
    )
    halos = [along_span(found[k].reshape(face), k % 2, k // 2) for k in range(4)]
    raw = [(HBM, x) for x in (inverse, rhs, upwind, south, north)]
    raw_scratch = [
        VMEM((elements, unknowns, unknowns), f32),
        VMEM((elements, unknowns, columns), f32),
        VMEM((elements, 3, unknowns, FACE), f32),
    ]
    fold_scratch = [VMEM((3 * depth, columns + 3 * WIDE), bf16), dma((elements, 5))]
    (own,) = call(
        fold_faces,
        [(VMEM, (CORES, elements, 3 * WIDE, half + 3 * WIDE), f32)],
        *raw,
        scratch=raw_scratch + [VMEM((3 * WIDE, depth), f32)] + fold_scratch,
        us=0,
        limit=MOST,
        after=found,
    )
    cores = lax.all_to_all(
        own, "sweep", 0, 0, axis_index_groups=[[i, i + 1] for i in range(0, devices, CORES)]
    )
    fc, fsn, fu, resp, step, *trace_blocks = call(
        chip_blocks,
        [
            (VMEM, (count, 3 * WIDE, half), f32),
            (VMEM, (count, 3 * WIDE, 6 * WIDE), bf16),
            (VMEM, (count, 3 * WIDE, 3 * WIDE), bf16),
            (VMEM, (count, 3 * WIDE, 3 * WIDE), bf16),
            (VMEM, (WIDE, WIDE), f32),
            (VMEM, (2 * WIDE, half), f32),
        ]
        + [(VMEM, (2 * WIDE, 2 * count * WIDE), bf16)] * 2,
        (VMEM, cores),
        scratch=[VMEM((3 * WIDE, WIDE), f32)],
        us=0,
    )
    steps = from_chips(step)[:-1]
    halo_split = (2 * count * WIDE, half)
    folded = [
        (VMEM, (depth, columns), f32),
        (VMEM, (depth, 6 * WIDE), bf16),
        (VMEM, (depth, 3 * WIDE), bf16),
    ]
    one_scratch = [VMEM((1,) + x.shape[1:], f32) for x in raw_scratch]
    one_scratch += [VMEM((depth, depth), f32), VMEM((3 * depth, columns + 3 * WIDE), bf16), dma((5,))]
    halo_parts = call(
        early_halos,
        [(VMEM, halo_split, bf16)] * 2,
        core, *[(HBM, halos[k]) for k in EARLY],
        scratch=[VMEM((len(EARLY), elements, FACE, half), f32), dma((len(EARLY),))],
        us=1,
    )
    folded_early = call(
        first_traces,
        [(VMEM, halo_split, bf16)] * 2 + [(VMEM, (WIDE, half), f32)] + folded,
        core, *held(trace_blocks), *[(HBM, halos[k]) for k in LATE], *raw, *held(halo_parts),
        scratch=[VMEM((len(LATE), elements, FACE, half), f32), dma((len(LATE),))] + one_scratch,
        us=2,
        aliases={9 + len(LATE): 0, 10 + len(LATE): 1},
    )
    halo_parts, out, early = folded_early[:2], folded_early[2], folded_early[3:]
    chips = from_chips(out)
    (faces,) = call(
        other_faces,
        [(VMEM, (count, 2 * WIDE, half), f32)],
        *held((fc, fsn, fu, *halo_parts)),
        us=2,
        after=steps,
    )
    last = call(
        next_faces,
        [(VMEM, (count, WIDE, half), f32)] * 2,
        core, *held((faces, resp, *chips, *steps)),
        scratch=[VMEM((WIDE, half), f32), VMEM((count, 2 * WIDE, half), f32)],
        us=1,
    )
    halos = [along_span(last[k], k, 0) for k in (1, 0)][::-1]
    late = call(
        fold_rest,
        folded * elements,
        core, *raw,
        scratch=one_scratch,
        us=10,
        after=last,
    )
    c, bsn, bu = [held([early[k], *late[k::3]]) for k in range(3)]
    (out,) = call(
        functools.partial(last_traces, slice(0, WIDE)),
        [(VMEM, (WIDE, half), f32)],
        core, *held((*trace_blocks, *halos[::-1])),
        scratch=[VMEM(halo_split, bf16)] * 2,
        us=1,
        after=late[:1],
    )
    lead, away = call(
        functools.partial(last_traces, slice(WIDE, 2 * WIDE)),
        [(VMEM, (WIDE, half), f32), (VMEM, (2, elements, WIDE, half), f32)],
        core, *held((*trace_blocks, *halos[::-1])),
        scratch=[VMEM(halo_split, bf16)] * 2,
        us=0,
        after=[out],
    )
    chips = from_chips(out)
    got = swap(away)
    parts = [
        call(
            functools.partial(field_without_inflow, other),
            [(VMEM, (elements, depth, half), f32)],
            core, *c, *bsn, *held(source),
            scratch=[VMEM((2 * WIDE, half), f32)],
            us=0 if other == 0 else 0,
            after=[out],
        )[0]
        for other, source in enumerate((halos, (got[0], got[1])))
    ]
    keep, send = call(
        inflow_of_cores,
        [(VMEM, (WIDE, half), f32)] * 2,
        core, *held((lead, resp, *chips, *steps)),
        us=20,
    )
    (field,) = call(
        whole_field,
        [(HBM, rhs.shape, f32)],
        core, *held((*parts, keep, swap(send))), *bu,
        scratch=[
            VMEM((WIDE, columns), f32),
            VMEM((elements, unknowns, columns), f32),
            dma((elements,)),
        ],
        us=1,
    )
    return by_row(field)


def solution(mesh):
    spec = P("sweep", "span", None, None)
    return jax.shard_map(
        per_device, mesh=mesh, in_specs=(spec,) * 6, out_specs=spec, check_vma=False
    )
```

```python
import functools

import jax
import jax.numpy as jnp
from jax import lax
from jax.experimental import pallas as pl
from jax.experimental.pallas import tpu as pltpu
from jax.sharding import PartitionSpec as P

VARS = 5
NODE = 5
FACE = VARS * NODE**2
WIDE = 128
SWEEPS = 2
CORES = 2
EARLY = (0, 1, 3)
LATE = (2,)
LIMIT = 24 * 1024 * 1024
MOST = 60 * 1024 * 1024
ANY = pl.ANY
HBM = pltpu.HBM
VMEM = pltpu.VMEM
SMEM = pltpu.SMEM


def face_runs(kind):
    if kind == "down":
        return [(var * NODE**3 + (NODE - 1) * NODE**2, NODE**2) for var in range(VARS)]
    b = NODE - 1 if kind == "high" else 0
    return [
        (var * NODE**3 + a * NODE**2 + b * NODE, NODE)
        for var in range(VARS)
        for a in range(NODE)
    ]


def split(x):
    top = x.astype(jnp.bfloat16)
    return top, (x - top.astype(jnp.float32)).astype(jnp.bfloat16)


def left(x):
    high, low = split(x)
    return jnp.concatenate([high, high, low], axis=1)


def right(x):
    high, low = split(x)
    return jnp.concatenate([high, low, high], axis=0)


def stacked(a, b):
    return jnp.dot(a, b, preferred_element_type=jnp.float32)


def padded(x, rows):
    short = rows - x.shape[0]
    return jnp.concatenate([x, jnp.zeros((short, x.shape[1]), x.dtype)], axis=0) if short else x


def call(kernel, outs, *args, scratch=(), us=1, after=(), limit=LIMIT, aliases=None):
    args = list(args) + [(ANY, x) for x in after]

    def body(*refs):
        given = len(args) - len(after)
        kernel(*refs[:given], *refs[len(args) :])

    return pl.pallas_call(
        body,
        out_shape=[jax.ShapeDtypeStruct(shape, kind) for _, shape, kind in outs],
        in_specs=[pl.BlockSpec(memory_space=space) for space, _ in args],
        out_specs=[pl.BlockSpec(memory_space=space) for space, _, _ in outs],
        scratch_shapes=list(scratch),
        input_output_aliases=aliases or {},
        compiler_params=pltpu.CompilerParams(vmem_limit_bytes=limit),
        cost_estimate=pl.CostEstimate(flops=int(us * 10**9), bytes_accessed=0, transcendentals=0),
        name=getattr(kernel, "func", kernel).__name__,
    )(*[array for _, array in args])


def start_faces(core_ref, field_ref, *refs):
    outs, sems = refs[:-1], refs[-1]
    half = outs[0].shape[-1]
    parts = []
    for k, out in enumerate(outs):
        own = core_ref[0] if k < 2 else 1 - core_ref[0]
        low = core_ref[2] if k % 2 == 0 else 1 - core_ref[2]
        part = pltpu.make_async_copy(
            field_ref.at[
                :, :, pl.ds((1 - low) * (NODE - 1) * NODE, NODE), :,
                pl.ds(pl.multiple_of(own * half, half), half),
            ],
            out,
            sems.at[k],
        )
        part.start()
        parts.append(part)
    for part in parts:
        part.wait()


def load_rows(pairs, sems):
    copies = []
    for k, (source, held) in enumerate(pairs):
        copies.append(pltpu.make_async_copy(source, held, sems.at[k]))
        copies[-1].start()
    return copies


def load_blocks(inv_ref, rhs_ref, up_ref, south_ref, north_ref, inv, rhs, blocks, sems):
    return [
        load_rows(
            [
                (inv_ref.at[e, :, 0, :], inv.at[e]),
                (rhs_ref.at[e, :, 0, :], rhs.at[e]),
                (south_ref.at[e, :, 0, :], blocks.at[e, 0]),
                (north_ref.at[e, :, 0, :], blocks.at[e, 1]),
                (up_ref.at[e, :, 0, :], blocks.at[e, 2]),
            ],
            sems.at[e],
        )
        for e in range(inv_ref.shape[0])
    ]


def fill_columns(e, depth, rhs, blocks, columns):
    wide = rhs.shape[2]
    columns[:, :wide] = right(padded(rhs[e], depth))
    for k in range(3):
        at = wide + k * WIDE
        block = right(padded(blocks[e, k], depth))
        columns[:, at : at + FACE] = block


def fold_faces(inv_ref, rhs_ref, up_ref, south_ref, north_ref, faces_ref,
               inv, rhs, blocks, rows, columns, sems):
    elements, depth, wide = inv.shape[0], rows.shape[1], rhs.shape[2]
    half = wide // CORES
    copies = load_blocks(inv_ref, rhs_ref, up_ref, south_ref, north_ref, inv, rhs, blocks, sems)
    rows[...] = jnp.zeros_like(rows)
    columns[...] = jnp.zeros_like(columns)
    for e in range(elements):
        copies[e][0].wait()
        for f, kind in enumerate(("down", "high", "low")):
            at = f * WIDE
            for first, length in face_runs(kind):
                rows[at : at + length, : inv.shape[2]] = inv[e, first : first + length, :]
                at += length
        for copy in copies[e][1:]:
            copy.wait()
        fill_columns(e, depth, rhs, blocks, columns)
        product = stacked(left(rows[...]), columns[...])
        for k in range(CORES):
            faces_ref[k, e, :, :half] = product[:, k * half : (k + 1) * half]
            faces_ref[k, e, :, half:] = product[:, wide:]


def fold_element(e, raw, outs, inv, rhs, blocks, rows, columns, sems):
    inv_ref, rhs_ref, up_ref, south_ref, north_ref = raw
    unknowns = inv.shape[1]
    depth, wide = rows.shape[1], rhs.shape[2]
    copies = load_rows(
        [
            (inv_ref.at[e, :, 0, :], inv.at[0]),
            (rhs_ref.at[e, :, 0, :], rhs.at[0]),
            (south_ref.at[e, :, 0, :], blocks.at[0, 0]),
            (north_ref.at[e, :, 0, :], blocks.at[0, 1]),
            (up_ref.at[e, :, 0, :], blocks.at[0, 2]),
        ],
        sems,
    )
    rows[...] = jnp.zeros_like(rows)
    columns[...] = jnp.zeros_like(columns)
    for copy in copies:
        copy.wait()
    rows[:unknowns, :unknowns] = inv[0]
    fill_columns(0, depth, rhs, blocks, columns)
    product = stacked(left(rows[...]), columns[...])
    c_ref, bsn_ref, bu_ref = outs
    c_ref[...] = product[:, :wide]
    bsn_ref[...] = left(product[:, wide : wide + 2 * WIDE])
    bu_ref[...] = left(product[:, wide + 2 * WIDE :])


def fold_rest(core_ref, *refs):
    raw, scratch = refs[:5], refs[-6:]
    outs = refs[5:-6]
    for e in range(len(outs) // 3 - 1, -1, -1):
        one = functools.partial(fold_element, e, raw, outs[3 * e : 3 * e + 3], *scratch)
        if e:
            one()
        else:
            pl.when(core_ref[0] == 1)(one)


def chip_blocks(faces_ref, fc_ref, fsn_ref, fu_ref, resp_ref, step_ref, const_ref, high_ref, low_ref, held):
    elements, half = faces_ref.shape[1], fc_ref.shape[2]
    count = CORES * elements
    for e in range(count):
        source = faces_ref.at[e // elements, e % elements]
        fc_ref[e] = source[:, :half]
        fsn_ref[e] = left(source[:, half : half + 2 * WIDE])
        own = source[:, half + 2 * WIDE :]
        fu_ref[e] = left(own)
        held[...] = -stacked(fu_ref[e], right(held[:WIDE, :])) if e else -own
        resp_ref[e] = left(held[...])
    step_ref[...] = held[:WIDE, :]
    high_ref[WIDE:, elements * 2 * WIDE :] = jnp.zeros_like(high_ref[WIDE:, elements * 2 * WIDE :])
    low_ref[WIDE:, elements * 2 * WIDE :] = jnp.zeros_like(low_ref[WIDE:, elements * 2 * WIDE :])
    for rows, last in ((slice(0, WIDE), count - 1), (slice(WIDE, 2 * WIDE), elements - 1)):
        passed = None
        for e in range(last, -1, -1):
            source = faces_ref.at[e // elements, e % elements]
            block = source[:WIDE, :]
            value = block if passed is None else stacked(left(passed), right(block))
            const = value[:, :half] if passed is None else const + value[:, :half]
            at = slice(e * 2 * WIDE, (e + 1) * 2 * WIDE)
            high_ref[rows, at], low_ref[rows, at] = split(value[:, half : half + 2 * WIDE])
            passed = -value[:, half + 2 * WIDE :]
        const_ref[rows, :] = const


def south_north(core_ref, k):
    return pl.multiple_of(((1 - core_ref[2]) if k == 0 else core_ref[2]) * WIDE, WIDE)


def traces(const, high, low, halo_high, halo_low):
    dot = functools.partial(jnp.dot, preferred_element_type=jnp.float32)
    return const - (dot(high, halo_high) + (dot(high, halo_low) + dot(low, halo_high)))


def take_halos(kinds, core_ref, halos, halo_high, halo_low, held, sems):
    elements = held.shape[1]
    copies = load_rows([(halo.at[:, :, 0, :], held.at[k]) for k, halo in enumerate(halos)], sems)
    for k, kind in enumerate(kinds):
        copies[k].wait()
        owner = core_ref[0] if kind < 2 else 1 - core_ref[0]
        for e in range(elements):
            row = 2 * WIDE * (owner * elements + e) + south_north(core_ref, kind % 2)
            at = pl.ds(pl.multiple_of(row, WIDE), WIDE)
            halo_high[at, :], halo_low[at, :] = split(padded(held[k, e], WIDE))


def early_halos(core_ref, *refs):
    take_halos(EARLY, core_ref, refs[: len(EARLY)], *refs[len(EARLY) :])


def first_traces(core_ref, const_ref, high_ref, low_ref, *refs):
    count = len(LATE)
    halos, raw, refs = refs[:count], refs[count : count + 5], refs[count + 7 :]
    halo_high, halo_low, out_ref, *outs = refs[:6]
    held, sems, *scratch = refs[6:]
    take_halos(LATE, core_ref, halos, halo_high, halo_low, held, sems)
    out_ref[...] = traces(
        const_ref[:WIDE, :], high_ref[:WIDE, :], low_ref[:WIDE, :], halo_high[...], halo_low[...]
    )
    pl.when(core_ref[0] == 0)(functools.partial(fold_element, 0, raw, outs, *scratch))


def other_faces(fc_ref, fsn_ref, fu_ref, halo_high, halo_low, faces_ref):
    trace = None
    for e in range(fc_ref.shape[0]):
        at = slice(2 * e * WIDE, 2 * (e + 1) * WIDE)
        high = halo_high[at, :]
        faces = fc_ref[e] - stacked(fsn_ref[e], jnp.concatenate([high, halo_low[at, :], high], axis=0))
        if e:
            faces = faces - stacked(fu_ref[e], right(trace))
        trace = faces[:WIDE]
        faces_ref[e] = faces[WIDE:]


def face_of(ref, e):
    return padded(ref[e * FACE : (e + 1) * FACE, :], WIDE)


def last_traces(rows, core_ref, const_ref, high_ref, low_ref, second_ref, first_ref, out_ref, *refs):
    halo_high, halo_low = refs[-2:]
    count = first_ref.shape[0] // FACE
    for e in range(count):
        for k, ref in enumerate((first_ref, second_ref)):
            at = pl.ds(pl.multiple_of(south_north(core_ref, k) + 2 * e * WIDE, WIDE), WIDE)
            halo_high[at, :], halo_low[at, :] = split(face_of(ref, e))
    out_ref[...] = traces(
        const_ref[rows, :], high_ref[rows, :], low_ref[rows, :], halo_high[...], halo_low[...]
    )
    if len(refs) > 2:
        elements = count // CORES

        def take(other):
            for e in range(elements):
                refs[0][0, e] = face_of(first_ref, other * elements + e)
                refs[0][1, e] = face_of(second_ref, other * elements + e)

        for k in range(CORES):
            pl.when(core_ref[0] == k)(functools.partial(take, 1 - k))


def through_chips(core_ref, inflow_ref, chips, steps):
    inflow_ref[...] = jnp.zeros_like(inflow_ref)
    for back in range(len(chips), 0, -1):

        @pl.when(core_ref[1] >= back)
        def _():
            if back == len(chips):
                inflow_ref[...] = chips[back - 1][...]
            else:
                passed = stacked(left(steps[back - 1][...]), right(inflow_ref[...]))
                inflow_ref[...] = chips[back - 1][...] + passed


def next_faces(core_ref, faces_ref, resp_ref, *refs):
    first_ref, second_ref, inflow_ref, both = refs[-4:]
    count = (len(refs) - 3) // 2
    through_chips(core_ref, inflow_ref, refs[:count], refs[count:-4])
    inflow = right(inflow_ref[...])
    first = pl.multiple_of(core_ref[2] * WIDE, WIDE)
    second = pl.multiple_of((1 - core_ref[2]) * WIDE, WIDE)
    for e in range(faces_ref.shape[0]):
        both[e] = faces_ref[e] + stacked(resp_ref[e, WIDE:, :], inflow)
    for e in range(faces_ref.shape[0]):
        first_ref[e * FACE : (e + 1) * FACE, :] = both[e, pl.ds(first, WIDE), :][:FACE]
        second_ref[e * FACE : (e + 1) * FACE, :] = both[e, pl.ds(second, WIDE), :][:FACE]


def inflow_of_cores(core_ref, lead_ref, resp_ref, *refs):
    keep_ref, send_ref = refs[-2:]
    count = (len(refs) - 1) // 2
    through_chips(core_ref, keep_ref, refs[:count], refs[count:-2])
    last = resp_ref.shape[0] // CORES - 1

    @pl.when(core_ref[0] == 0)
    def _():
        send_ref[...] = lead_ref[...] + stacked(resp_ref[last, :WIDE, :], right(keep_ref[...]))

    @pl.when(core_ref[0] == 1)
    def _():
        send_ref[...] = keep_ref[...]
        keep_ref[...] = lead_ref[...] + stacked(resp_ref[last, :WIDE, :], right(send_ref[...]))


def join(core_ref, keep_ref, got_ref, inflow_ref):
    half = keep_ref.shape[1]

    @pl.when(core_ref[0] == 0)
    def _():
        inflow_ref[:, :half] = keep_ref[...]
        inflow_ref[:, half:] = got_ref[...]

    @pl.when(core_ref[0] == 1)
    def _():
        inflow_ref[:, :half] = got_ref[...]
        inflow_ref[:, half:] = keep_ref[...]


def field_without_inflow(other, core_ref, *refs):
    first_ref, second_ref, p_ref, halo = refs[-4:]
    elements, half = p_ref.shape[0], p_ref.shape[2]
    c_refs, bsn_refs = refs[: elements + 1], refs[elements + 1 : 2 * elements + 2]
    at = pl.ds(pl.multiple_of((1 - core_ref[0] if other else core_ref[0]) * half, half), half)
    for e in range(elements):
        for k, ref in enumerate((first_ref, second_ref)):
            rows = pl.ds(south_north(core_ref, k), WIDE)
            if other:
                halo[rows, :] = ref[e]
                continue

            def take(own):
                halo[rows, :] = face_of(ref, own * elements + e)

            for c in range(CORES):
                pl.when(core_ref[0] == c)(functools.partial(take, c))
        halos = right(halo[...])

        def place(c_ref, bsn_ref):
            p_ref[e] = c_ref[:, at] - stacked(bsn_ref[...], halos)

        by_core(core_ref, e, place, c_refs, bsn_refs)


def by_core(core_ref, e, use, *stacks):
    if e:
        use(*[refs[e + 1] for refs in stacks])
    else:
        for k in range(CORES):
            pl.when(core_ref[0] == k)(functools.partial(use, *[refs[k] for refs in stacks]))


def whole_field(core_ref, own_ref, other_ref, keep_ref, got_ref, *refs):
    bu_refs, (out_ref, inflow_ref, held, sems) = refs[:-4], refs[-4:]
    join(core_ref, keep_ref, got_ref, inflow_ref)
    elements, unknowns = held.shape[:2]
    half = keep_ref.shape[1]
    copies = []
    for e in range(elements):
        if e:
            at = 0
            for first, length in face_runs("down"):
                inflow_ref[at : at + length, :] = held[e - 1, first : first + length, :]
                at += length
        inflow = right(inflow_ref[...])

        def place(own, bu_ref):
            change = stacked(bu_ref[...], inflow)[:unknowns]
            for k in range(CORES):
                part = own_ref if k == own else other_ref
                at = slice(k * half, (k + 1) * half)
                held[e, :, at] = part[e, :unknowns, :] - change[:, at]

        for k in range(CORES):
            pl.when(core_ref[0] == k)(functools.partial(place, k, bu_refs[e + 1 if e else k]))
        copy = pltpu.make_async_copy(held.at[e], out_ref.at[e, :, 0, :], sems.at[e])
        copy.start()
        copies.append(copy)
    for copy in copies:
        copy.wait()


def ring(axis, by):
    count = lax.axis_size(axis)
    return [(i, (i + by) % count) for i in range(count)]


def per_device(right_side, start_field, block_inverse, upwind_block, south_block, north_block):
    by_row = lambda x: x.transpose(0, 2, 1, 3)
    rhs, start, inverse, upwind, south, north = map(
        by_row, (right_side, start_field, block_inverse, upwind_block, south_block, north_block)
    )
    elements, unknowns, _, columns = rhs.shape
    depth = -(-unknowns // 128) * 128
    half = columns // CORES
    count = CORES * elements
    devices, spans = lax.axis_size("sweep"), lax.axis_size("span")
    place = lax.axis_index("sweep")
    odd = lax.axis_index("span") % 2
    where = jnp.stack([place % CORES, place // CORES, odd]).astype(jnp.int32)
    dma = pltpu.SemaphoreType.DMA
    f32, bf16 = jnp.float32, jnp.bfloat16
    core = (SMEM, where)
    face = (elements, FACE, 1, half)

    def held(arrays):
        return [(VMEM, x) for x in arrays]

    def swap(x):
        return lax.ppermute(x, "sweep", [(i, i ^ 1) for i in range(devices)])

    def from_chips(x):
        return [
            lax.ppermute(x, "sweep", ring("sweep", CORES * back))
            for back in range(1, devices // CORES)
        ]

    def along_span(x, second, other_core):
        pairs = []
        for i in range(devices):
            for j in range(spans):
                by = 1 if (j + second) % 2 == 0 else -1
                pairs.append((i * spans + j, (i ^ other_core) * spans + (j + by) % spans))
        return lax.ppermute(x, ("sweep", "span"), pairs)

    runs = start.reshape(elements, NODE**2, VARS * NODE, 1, columns)
    found = call(
        start_faces,
        [(VMEM, (elements, NODE**2, NODE, 1, half), f32)] * 4,
        core, (HBM, runs),
        scratch=[dma((4,))],
    )
    halos = [along_span(found[k].reshape(face), k % 2, k // 2) for k in range(4)]
    raw = [(HBM, x) for x in (inverse, rhs, upwind, south, north)]
    raw_scratch = [
        VMEM((elements, unknowns, unknowns), f32),
        VMEM((elements, unknowns, columns), f32),
        VMEM((elements, 3, unknowns, FACE), f32),
    ]
    fold_scratch = [VMEM((3 * depth, columns + 3 * WIDE), bf16), dma((elements, 5))]
    (own,) = call(
        fold_faces,
        [(VMEM, (CORES, elements, 3 * WIDE, half + 3 * WIDE), f32)],
        *raw,
        scratch=raw_scratch + [VMEM((3 * WIDE, depth), f32)] + fold_scratch,
        us=0,
        limit=MOST,
        after=found,
    )
    cores = lax.all_to_all(
        own, "sweep", 0, 0, axis_index_groups=[[i, i + 1] for i in range(0, devices, CORES)]
    )
    fc, fsn, fu, resp, step, *trace_blocks = call(
        chip_blocks,
        [
            (VMEM, (count, 3 * WIDE, half), f32),
            (VMEM, (count, 3 * WIDE, 6 * WIDE), bf16),
            (VMEM, (count, 3 * WIDE, 3 * WIDE), bf16),
            (VMEM, (count, 3 * WIDE, 3 * WIDE), bf16),
            (VMEM, (WIDE, WIDE), f32),
            (VMEM, (2 * WIDE, half), f32),
        ]
        + [(VMEM, (2 * WIDE, 2 * count * WIDE), bf16)] * 2,
        (VMEM, cores),
        scratch=[VMEM((3 * WIDE, WIDE), f32)],
        us=0,
    )
    steps = from_chips(step)[:-1]
    halo_split = (2 * count * WIDE, half)
    folded = [
        (VMEM, (depth, columns), f32),
        (VMEM, (depth, 6 * WIDE), bf16),
        (VMEM, (depth, 3 * WIDE), bf16),
    ]
    one_scratch = [VMEM((1,) + x.shape[1:], f32) for x in raw_scratch]
    one_scratch += [VMEM((depth, depth), f32), VMEM((3 * depth, columns + 3 * WIDE), bf16), dma((5,))]
    halo_parts = call(
        early_halos,
        [(VMEM, halo_split, bf16)] * 2,
        core, *[(HBM, halos[k]) for k in EARLY],
        scratch=[VMEM((len(EARLY), elements, FACE, half), f32), dma((len(EARLY),))],
        us=1,
    )
    folded_early = call(
        first_traces,
        [(VMEM, halo_split, bf16)] * 2 + [(VMEM, (WIDE, half), f32)] + folded,
        core, *held(trace_blocks), *[(HBM, halos[k]) for k in LATE], *raw, *held(halo_parts),
        scratch=[VMEM((len(LATE), elements, FACE, half), f32), dma((len(LATE),))] + one_scratch,
        us=2,
        aliases={9 + len(LATE): 0, 10 + len(LATE): 1},
    )
    halo_parts, out, early = folded_early[:2], folded_early[2], folded_early[3:]
    chips = from_chips(out)
    (faces,) = call(
        other_faces,
        [(VMEM, (count, 2 * WIDE, half), f32)],
        *held((fc, fsn, fu, *halo_parts)),
        us=2,
        after=steps,
    )
    last = call(
        next_faces,
        [(VMEM, (count * FACE, half), f32)] * 2,
        core, *held((faces, resp, *chips, *steps)),
        scratch=[VMEM((WIDE, half), f32), VMEM((count, 2 * WIDE, half), f32)],
        us=1,
    )
    halos = [along_span(last[k], k, 0) for k in (1, 0)][::-1]
    late = call(
        fold_rest,
        folded * elements,
        core, *raw,
        scratch=one_scratch,
        us=10,
        after=last,
    )
    c, bsn, bu = [held([early[k], *late[k::3]]) for k in range(3)]
    (out,) = call(
        functools.partial(last_traces, slice(0, WIDE)),
        [(VMEM, (WIDE, half), f32)],
        core, *held((*trace_blocks, *halos[::-1])),
        scratch=[VMEM(halo_split, bf16)] * 2,
        us=1,
        after=late[:1],
    )
    lead, away = call(
        functools.partial(last_traces, slice(WIDE, 2 * WIDE)),
        [(VMEM, (WIDE, half), f32), (VMEM, (2, elements, WIDE, half), f32)],
        core, *held((*trace_blocks, *halos[::-1])),
        scratch=[VMEM(halo_split, bf16)] * 2,
        us=0,
        after=[out],
    )
    chips = from_chips(out)
    got = swap(away)
    parts = [
        call(
            functools.partial(field_without_inflow, other),
            [(VMEM, (elements, depth, half), f32)],
            core, *c, *bsn, *held(source),
            scratch=[VMEM((2 * WIDE, half), f32)],
            us=0 if other == 0 else 0,
            after=[out],
        )[0]
        for other, source in enumerate((halos, (got[0], got[1])))
    ]
    keep, send = call(
        inflow_of_cores,
        [(VMEM, (WIDE, half), f32)] * 2,
        core, *held((lead, resp, *chips, *steps)),
        us=20,
    )
    (field,) = call(
        whole_field,
        [(HBM, rhs.shape, f32)],
        core, *held((*parts, keep, swap(send))), *bu,
        scratch=[
            VMEM((WIDE, columns), f32),
            VMEM((elements, unknowns, columns), f32),
            dma((elements,)),
        ],
        us=1,
    )
    return by_row(field)


def solution(mesh):
    spec = P("sweep", "span", None, None)
    return jax.shard_map(
        per_device, mesh=mesh, in_specs=(spec,) * 6, out_specs=spec, check_vma=False
    )
```

```python
import functools

import jax
import jax.numpy as jnp
from jax import lax
from jax.experimental import pallas as pl
from jax.experimental.pallas import tpu as pltpu
from jax.sharding import PartitionSpec as P

VARS = 5
NODE = 5
FACE = VARS * NODE**2
WIDE = 128
SWEEPS = 2
CORES = 2
EARLY = (0, 3, 1)
LATE = (2,)
LIMIT = 24 * 1024 * 1024
MOST = 60 * 1024 * 1024
ANY = pl.ANY
HBM = pltpu.HBM
VMEM = pltpu.VMEM
SMEM = pltpu.SMEM


def face_runs(kind):
    if kind == "down":
        return [(var * NODE**3 + (NODE - 1) * NODE**2, NODE**2) for var in range(VARS)]
    b = NODE - 1 if kind == "high" else 0
    return [
        (var * NODE**3 + a * NODE**2 + b * NODE, NODE)
        for var in range(VARS)
        for a in range(NODE)
    ]


def split(x):
    top = x.astype(jnp.bfloat16)
    return top, (x - top.astype(jnp.float32)).astype(jnp.bfloat16)


def left(x):
    high, low = split(x)
    return jnp.concatenate([high, high, low], axis=1)


def right(x):
    high, low = split(x)
    return jnp.concatenate([high, low, high], axis=0)


def stacked(a, b):
    return jnp.dot(a, b, preferred_element_type=jnp.float32)


def padded(x, rows):
    short = rows - x.shape[0]
    return jnp.concatenate([x, jnp.zeros((short, x.shape[1]), x.dtype)], axis=0) if short else x


def call(kernel, outs, *args, scratch=(), us=1, after=(), limit=LIMIT, aliases=None):
    args = list(args) + [(ANY, x) for x in after]

    def body(*refs):
        given = len(args) - len(after)
        kernel(*refs[:given], *refs[len(args) :])

    return pl.pallas_call(
        body,
        out_shape=[jax.ShapeDtypeStruct(shape, kind) for _, shape, kind in outs],
        in_specs=[pl.BlockSpec(memory_space=space) for space, _ in args],
        out_specs=[pl.BlockSpec(memory_space=space) for space, _, _ in outs],
        scratch_shapes=list(scratch),
        input_output_aliases=aliases or {},
        compiler_params=pltpu.CompilerParams(vmem_limit_bytes=limit),
        cost_estimate=pl.CostEstimate(flops=int(us * 10**9), bytes_accessed=0, transcendentals=0),
        name=getattr(kernel, "func", kernel).__name__,
    )(*[array for _, array in args])


def start_faces(core_ref, field_ref, *refs):
    outs, sems = refs[:-1], refs[-1]
    half = outs[0].shape[-1]
    parts = []
    for k, out in enumerate(outs):
        own = core_ref[0] if k < 2 else 1 - core_ref[0]
        low = core_ref[2] if k % 2 == 0 else 1 - core_ref[2]
        part = pltpu.make_async_copy(
            field_ref.at[
                :, :, pl.ds((1 - low) * (NODE - 1) * NODE, NODE), :,
                pl.ds(pl.multiple_of(own * half, half), half),
            ],
            out,
            sems.at[k],
        )
        part.start()
        parts.append(part)
    for part in parts:
        part.wait()


def load_rows(pairs, sems):
    copies = []
    for k, (source, held) in enumerate(pairs):
        copies.append(pltpu.make_async_copy(source, held, sems.at[k]))
        copies[-1].start()
    return copies


def load_blocks(inv_ref, rhs_ref, up_ref, south_ref, north_ref, inv, rhs, blocks, sems):
    return [
        load_rows(
            [
                (inv_ref.at[e, :, 0, :], inv.at[e]),
                (rhs_ref.at[e, :, 0, :], rhs.at[e]),
                (south_ref.at[e, :, 0, :], blocks.at[e, 0]),
                (north_ref.at[e, :, 0, :], blocks.at[e, 1]),
                (up_ref.at[e, :, 0, :], blocks.at[e, 2]),
            ],
            sems.at[e],
        )
        for e in range(inv_ref.shape[0])
    ]


def fill_columns(e, depth, rhs, blocks, columns):
    wide = rhs.shape[2]
    columns[:, :wide] = right(padded(rhs[e], depth))
    for k in range(3):
        at = wide + k * WIDE
        block = right(padded(blocks[e, k], depth))
        columns[:, at : at + FACE] = block


def fold_faces(inv_ref, rhs_ref, up_ref, south_ref, north_ref, faces_ref,
               inv, rhs, blocks, rows, columns, sems):
    elements, depth, wide = inv.shape[0], rows.shape[1], rhs.shape[2]
    half = wide // CORES
    copies = load_blocks(inv_ref, rhs_ref, up_ref, south_ref, north_ref, inv, rhs, blocks, sems)
    rows[...] = jnp.zeros_like(rows)
    columns[...] = jnp.zeros_like(columns)
    for e in range(elements):
        copies[e][0].wait()
        for f, kind in enumerate(("down", "high", "low")):
            at = f * WIDE
            for first, length in face_runs(kind):
                rows[at : at + length, : inv.shape[2]] = inv[e, first : first + length, :]
                at += length
        for copy in copies[e][1:]:
            copy.wait()
        fill_columns(e, depth, rhs, blocks, columns)
        product = stacked(left(rows[...]), columns[...])
        for k in range(CORES):
            faces_ref[k, e, :, :half] = product[:, k * half : (k + 1) * half]
            faces_ref[k, e, :, half:] = product[:, wide:]


def fold_element(e, raw, outs, inv, rhs, blocks, rows, columns, sems):
    inv_ref, rhs_ref, up_ref, south_ref, north_ref = raw
    unknowns = inv.shape[1]
    depth, wide = rows.shape[1], rhs.shape[2]
    copies = load_rows(
        [
            (inv_ref.at[e, :, 0, :], inv.at[0]),
            (rhs_ref.at[e, :, 0, :], rhs.at[0]),
            (south_ref.at[e, :, 0, :], blocks.at[0, 0]),
            (north_ref.at[e, :, 0, :], blocks.at[0, 1]),
            (up_ref.at[e, :, 0, :], blocks.at[0, 2]),
        ],
        sems,
    )
    rows[...] = jnp.zeros_like(rows)
    columns[...] = jnp.zeros_like(columns)
    for copy in copies:
        copy.wait()
    rows[:unknowns, :unknowns] = inv[0]
    fill_columns(0, depth, rhs, blocks, columns)
    product = stacked(left(rows[...]), columns[...])
    c_ref, bsn_ref, bu_ref = outs
    c_ref[...] = product[:, :wide]
    bsn_ref[...] = left(product[:, wide : wide + 2 * WIDE])
    bu_ref[...] = left(product[:, wide + 2 * WIDE :])


def fold_rest(core_ref, *refs):
    raw, scratch = refs[:5], refs[-6:]
    outs = refs[5:-6]
    for e in range(len(outs) // 3 - 1, -1, -1):
        one = functools.partial(fold_element, e, raw, outs[3 * e : 3 * e + 3], *scratch)
        if e:
            one()
        else:
            pl.when(core_ref[0] == 1)(one)


def chip_blocks(faces_ref, fc_ref, fsn_ref, fu_ref, resp_ref, step_ref, const_ref, high_ref, low_ref, held):
    elements, half = faces_ref.shape[1], fc_ref.shape[2]
    count = CORES * elements
    for e in range(count):
        source = faces_ref.at[e // elements, e % elements]
        fc_ref[e] = source[:, :half]
        fsn_ref[e] = left(source[:, half : half + 2 * WIDE])
        own = source[:, half + 2 * WIDE :]
        fu_ref[e] = left(own)
        held[...] = -stacked(fu_ref[e], right(held[:WIDE, :])) if e else -own
        resp_ref[e] = left(held[...])
    step_ref[...] = held[:WIDE, :]
    high_ref[WIDE:, elements * 2 * WIDE :] = jnp.zeros_like(high_ref[WIDE:, elements * 2 * WIDE :])
    low_ref[WIDE:, elements * 2 * WIDE :] = jnp.zeros_like(low_ref[WIDE:, elements * 2 * WIDE :])
    for rows, last in ((slice(0, WIDE), count - 1), (slice(WIDE, 2 * WIDE), elements - 1)):
        passed = None
        for e in range(last, -1, -1):
            source = faces_ref.at[e // elements, e % elements]
            block = source[:WIDE, :]
            value = block if passed is None else stacked(left(passed), right(block))
            const = value[:, :half] if passed is None else const + value[:, :half]
            at = slice(e * 2 * WIDE, (e + 1) * 2 * WIDE)
            high_ref[rows, at], low_ref[rows, at] = split(value[:, half : half + 2 * WIDE])
            passed = -value[:, half + 2 * WIDE :]
        const_ref[rows, :] = const


def south_north(core_ref, k):
    return pl.multiple_of(((1 - core_ref[2]) if k == 0 else core_ref[2]) * WIDE, WIDE)


def traces(const, high, low, halo_high, halo_low):
    dot = functools.partial(jnp.dot, preferred_element_type=jnp.float32)
    return const - (dot(high, halo_high) + (dot(high, halo_low) + dot(low, halo_high)))


def take_halos(kinds, core_ref, halos, halo_high, halo_low, held, sems):
    elements = held.shape[1]
    copies = load_rows([(halo.at[:, :, 0, :], held.at[k]) for k, halo in enumerate(halos)], sems)
    for k, kind in enumerate(kinds):
        copies[k].wait()
        owner = core_ref[0] if kind < 2 else 1 - core_ref[0]
        for e in range(elements):
            row = 2 * WIDE * (owner * elements + e) + south_north(core_ref, kind % 2)
            at = pl.ds(pl.multiple_of(row, WIDE), WIDE)
            halo_high[at, :], halo_low[at, :] = split(padded(held[k, e], WIDE))


def early_halos(core_ref, *refs):
    take_halos(EARLY, core_ref, refs[: len(EARLY)], *refs[len(EARLY) :])


def first_traces(core_ref, const_ref, high_ref, low_ref, *refs):
    count = len(LATE)
    halos, raw, refs = refs[:count], refs[count : count + 5], refs[count + 7 :]
    halo_high, halo_low, out_ref, *outs = refs[:6]
    held, sems, *scratch = refs[6:]
    take_halos(LATE, core_ref, halos, halo_high, halo_low, held, sems)
    out_ref[...] = traces(
        const_ref[:WIDE, :], high_ref[:WIDE, :], low_ref[:WIDE, :], halo_high[...], halo_low[...]
    )
    pl.when(core_ref[0] == 0)(functools.partial(fold_element, 0, raw, outs, *scratch))


def other_faces(fc_ref, fsn_ref, fu_ref, halo_high, halo_low, faces_ref):
    trace = None
    for e in range(fc_ref.shape[0]):
        at = slice(2 * e * WIDE, 2 * (e + 1) * WIDE)
        high = halo_high[at, :]
        faces = fc_ref[e] - stacked(fsn_ref[e], jnp.concatenate([high, halo_low[at, :], high], axis=0))
        if e:
            faces = faces - stacked(fu_ref[e], right(trace))
        trace = faces[:WIDE]
        faces_ref[e] = faces[WIDE:]


def face_of(ref, e):
    return padded(ref[e * FACE : (e + 1) * FACE, :], WIDE)


def last_traces(rows, core_ref, const_ref, high_ref, low_ref, second_ref, first_ref, out_ref, *refs):
    halo_high, halo_low = refs[-2:]
    count = first_ref.shape[0] // FACE
    for e in range(count):
        for k, ref in enumerate((first_ref, second_ref)):
            at = pl.ds(pl.multiple_of(south_north(core_ref, k) + 2 * e * WIDE, WIDE), WIDE)
            halo_high[at, :], halo_low[at, :] = split(face_of(ref, e))
    out_ref[...] = traces(
        const_ref[rows, :], high_ref[rows, :], low_ref[rows, :], halo_high[...], halo_low[...]
    )
    if len(refs) > 2:
        elements = count // CORES

        def take(other):
            for e in range(elements):
                refs[0][0, e] = face_of(first_ref, other * elements + e)
                refs[0][1, e] = face_of(second_ref, other * elements + e)

        for k in range(CORES):
            pl.when(core_ref[0] == k)(functools.partial(take, 1 - k))


def through_chips(core_ref, inflow_ref, chips, steps):
    inflow_ref[...] = jnp.zeros_like(inflow_ref)
    for back in range(len(chips), 0, -1):

        @pl.when(core_ref[1] >= back)
        def _():
            if back == len(chips):
                inflow_ref[...] = chips[back - 1][...]
            else:
                passed = stacked(left(steps[back - 1][...]), right(inflow_ref[...]))
                inflow_ref[...] = chips[back - 1][...] + passed


def next_faces(core_ref, faces_ref, resp_ref, *refs):
    first_ref, second_ref, inflow_ref, both = refs[-4:]
    count = (len(refs) - 3) // 2
    through_chips(core_ref, inflow_ref, refs[:count], refs[count:-4])
    inflow = right(inflow_ref[...])
    first = pl.multiple_of(core_ref[2] * WIDE, WIDE)
    second = pl.multiple_of((1 - core_ref[2]) * WIDE, WIDE)
    for e in range(faces_ref.shape[0]):
        both[e] = faces_ref[e] + stacked(resp_ref[e, WIDE:, :], inflow)
    for e in range(faces_ref.shape[0]):
        first_ref[e * FACE : (e + 1) * FACE, :] = both[e, pl.ds(first, WIDE), :][:FACE]
        second_ref[e * FACE : (e + 1) * FACE, :] = both[e, pl.ds(second, WIDE), :][:FACE]


def inflow_of_cores(core_ref, lead_ref, resp_ref, *refs):
    keep_ref, send_ref = refs[-2:]
    count = (len(refs) - 1) // 2
    through_chips(core_ref, keep_ref, refs[:count], refs[count:-2])
    last = resp_ref.shape[0] // CORES - 1

    @pl.when(core_ref[0] == 0)
    def _():
        send_ref[...] = lead_ref[...] + stacked(resp_ref[last, :WIDE, :], right(keep_ref[...]))

    @pl.when(core_ref[0] == 1)
    def _():
        send_ref[...] = keep_ref[...]
        keep_ref[...] = lead_ref[...] + stacked(resp_ref[last, :WIDE, :], right(send_ref[...]))


def join(core_ref, keep_ref, got_ref, inflow_ref):
    half = keep_ref.shape[1]

    @pl.when(core_ref[0] == 0)
    def _():
        inflow_ref[:, :half] = keep_ref[...]
        inflow_ref[:, half:] = got_ref[...]

    @pl.when(core_ref[0] == 1)
    def _():
        inflow_ref[:, :half] = got_ref[...]
        inflow_ref[:, half:] = keep_ref[...]


def field_without_inflow(other, core_ref, *refs):
    first_ref, second_ref, p_ref, halo = refs[-4:]
    elements, half = p_ref.shape[0], p_ref.shape[2]
    c_refs, bsn_refs = refs[: elements + 1], refs[elements + 1 : 2 * elements + 2]
    at = pl.ds(pl.multiple_of((1 - core_ref[0] if other else core_ref[0]) * half, half), half)
    for e in range(elements):
        for k, ref in enumerate((first_ref, second_ref)):
            rows = pl.ds(south_north(core_ref, k), WIDE)
            if other:
                halo[rows, :] = ref[e]
                continue

            def take(own):
                halo[rows, :] = face_of(ref, own * elements + e)

            for c in range(CORES):
                pl.when(core_ref[0] == c)(functools.partial(take, c))
        halos = right(halo[...])

        def place(c_ref, bsn_ref):
            p_ref[e] = c_ref[:, at] - stacked(bsn_ref[...], halos)

        by_core(core_ref, e, place, c_refs, bsn_refs)


def by_core(core_ref, e, use, *stacks):
    if e:
        use(*[refs[e + 1] for refs in stacks])
    else:
        for k in range(CORES):
            pl.when(core_ref[0] == k)(functools.partial(use, *[refs[k] for refs in stacks]))


def whole_field(core_ref, own_ref, other_ref, keep_ref, got_ref, *refs):
    bu_refs, (out_ref, inflow_ref, held, sems) = refs[:-4], refs[-4:]
    join(core_ref, keep_ref, got_ref, inflow_ref)
    elements, unknowns = held.shape[:2]
    half = keep_ref.shape[1]
    copies = []
    for e in range(elements):
        if e:
            at = 0
            for first, length in face_runs("down"):
                inflow_ref[at : at + length, :] = held[e - 1, first : first + length, :]
                at += length
        inflow = right(inflow_ref[...])

        def place(own, bu_ref):
            change = stacked(bu_ref[...], inflow)[:unknowns]
            for k in range(CORES):
                part = own_ref if k == own else other_ref
                at = slice(k * half, (k + 1) * half)
                held[e, :, at] = part[e, :unknowns, :] - change[:, at]

        for k in range(CORES):
            pl.when(core_ref[0] == k)(functools.partial(place, k, bu_refs[e + 1 if e else k]))
        copy = pltpu.make_async_copy(held.at[e], out_ref.at[e, :, 0, :], sems.at[e])
        copy.start()
        copies.append(copy)
    for copy in copies:
        copy.wait()


def ring(axis, by):
    count = lax.axis_size(axis)
    return [(i, (i + by) % count) for i in range(count)]


def per_device(right_side, start_field, block_inverse, upwind_block, south_block, north_block):
    by_row = lambda x: x.transpose(0, 2, 1, 3)
    rhs, start, inverse, upwind, south, north = map(
        by_row, (right_side, start_field, block_inverse, upwind_block, south_block, north_block)
    )
    elements, unknowns, _, columns = rhs.shape
    depth = -(-unknowns // 128) * 128
    half = columns // CORES
    count = CORES * elements
    devices, spans = lax.axis_size("sweep"), lax.axis_size("span")
    place = lax.axis_index("sweep")
    odd = lax.axis_index("span") % 2
    where = jnp.stack([place % CORES, place // CORES, odd]).astype(jnp.int32)
    dma = pltpu.SemaphoreType.DMA
    f32, bf16 = jnp.float32, jnp.bfloat16
    core = (SMEM, where)
    face = (elements, FACE, 1, half)

    def held(arrays):
        return [(VMEM, x) for x in arrays]

    def swap(x):
        return lax.ppermute(x, "sweep", [(i, i ^ 1) for i in range(devices)])

    def from_chips(x):
        return [
            lax.ppermute(x, "sweep", ring("sweep", CORES * back))
            for back in range(1, devices // CORES)
        ]

    def along_span(x, second, other_core):
        pairs = []
        for i in range(devices):
            for j in range(spans):
                by = 1 if (j + second) % 2 == 0 else -1
                pairs.append((i * spans + j, (i ^ other_core) * spans + (j + by) % spans))
        return lax.ppermute(x, ("sweep", "span"), pairs)

    runs = start.reshape(elements, NODE**2, VARS * NODE, 1, columns)
    found = call(
        start_faces,
        [(VMEM, (elements, NODE**2, NODE, 1, half), f32)] * 4,
        core, (HBM, runs),
        scratch=[dma((4,))],
    )
    halos = [along_span(found[k].reshape(face), k % 2, k // 2) for k in range(4)]
    raw = [(HBM, x) for x in (inverse, rhs, upwind, south, north)]
    raw_scratch = [
        VMEM((elements, unknowns, unknowns), f32),
        VMEM((elements, unknowns, columns), f32),
        VMEM((elements, 3, unknowns, FACE), f32),
    ]
    fold_scratch = [VMEM((3 * depth, columns + 3 * WIDE), bf16), dma((elements, 5))]
    (own,) = call(
        fold_faces,
        [(VMEM, (CORES, elements, 3 * WIDE, half + 3 * WIDE), f32)],
        *raw,
        scratch=raw_scratch + [VMEM((3 * WIDE, depth), f32)] + fold_scratch,
        us=0,
        limit=MOST,
        after=found,
    )
    cores = lax.all_to_all(
        own, "sweep", 0, 0, axis_index_groups=[[i, i + 1] for i in range(0, devices, CORES)]
    )
    fc, fsn, fu, resp, step, *trace_blocks = call(
        chip_blocks,
        [
            (VMEM, (count, 3 * WIDE, half), f32),
            (VMEM, (count, 3 * WIDE, 6 * WIDE), bf16),
            (VMEM, (count, 3 * WIDE, 3 * WIDE), bf16),
            (VMEM, (count, 3 * WIDE, 3 * WIDE), bf16),
            (VMEM, (WIDE, WIDE), f32),
            (VMEM, (2 * WIDE, half), f32),
        ]
        + [(VMEM, (2 * WIDE, 2 * count * WIDE), bf16)] * 2,
        (VMEM, cores),
        scratch=[VMEM((3 * WIDE, WIDE), f32)],
        us=0,
    )
    steps = from_chips(step)[:-1]
    halo_split = (2 * count * WIDE, half)
    folded = [
        (VMEM, (depth, columns), f32),
        (VMEM, (depth, 6 * WIDE), bf16),
        (VMEM, (depth, 3 * WIDE), bf16),
    ]
    one_scratch = [VMEM((1,) + x.shape[1:], f32) for x in raw_scratch]
    one_scratch += [VMEM((depth, depth), f32), VMEM((3 * depth, columns + 3 * WIDE), bf16), dma((5,))]
    halo_parts = call(
        early_halos,
        [(VMEM, halo_split, bf16)] * 2,
        core, *[(HBM, halos[k]) for k in EARLY],
        scratch=[VMEM((len(EARLY), elements, FACE, half), f32), dma((len(EARLY),))],
        us=1,
    )
    folded_early = call(
        first_traces,
        [(VMEM, halo_split, bf16)] * 2 + [(VMEM, (WIDE, half), f32)] + folded,
        core, *held(trace_blocks), *[(HBM, halos[k]) for k in LATE], *raw, *held(halo_parts),
        scratch=[VMEM((len(LATE), elements, FACE, half), f32), dma((len(LATE),))] + one_scratch,
        us=2,
        aliases={9 + len(LATE): 0, 10 + len(LATE): 1},
    )
    halo_parts, out, early = folded_early[:2], folded_early[2], folded_early[3:]
    chips = from_chips(out)
    (faces,) = call(
        other_faces,
        [(VMEM, (count, 2 * WIDE, half), f32)],
        *held((fc, fsn, fu, *halo_parts)),
        us=2,
        after=steps,
    )
    last = call(
        next_faces,
        [(VMEM, (count * FACE, half), f32)] * 2,
        core, *held((faces, resp, *chips, *steps)),
        scratch=[VMEM((WIDE, half), f32), VMEM((count, 2 * WIDE, half), f32)],
        us=1,
    )
    halos = [along_span(last[k], k, 0) for k in (1, 0)][::-1]
    late = call(
        fold_rest,
        folded * elements,
        core, *raw,
        scratch=one_scratch,
        us=10,
        after=last,
    )
    c, bsn, bu = [held([early[k], *late[k::3]]) for k in range(3)]
    (out,) = call(
        functools.partial(last_traces, slice(0, WIDE)),
        [(VMEM, (WIDE, half), f32)],
        core, *held((*trace_blocks, *halos[::-1])),
        scratch=[VMEM(halo_split, bf16)] * 2,
        us=1,
        after=late[:1],
    )
    lead, away = call(
        functools.partial(last_traces, slice(WIDE, 2 * WIDE)),
        [(VMEM, (WIDE, half), f32), (VMEM, (2, elements, WIDE, half), f32)],
        core, *held((*trace_blocks, *halos[::-1])),
        scratch=[VMEM(halo_split, bf16)] * 2,
        us=0,
        after=[out],
    )
    chips = from_chips(out)
    got = swap(away)
    parts = [
        call(
            functools.partial(field_without_inflow, other),
            [(VMEM, (elements, depth, half), f32)],
            core, *c, *bsn, *held(source),
            scratch=[VMEM((2 * WIDE, half), f32)],
            us=0 if other == 0 else 0,
            after=[out],
        )[0]
        for other, source in enumerate((halos, (got[0], got[1])))
    ]
    keep, send = call(
        inflow_of_cores,
        [(VMEM, (WIDE, half), f32)] * 2,
        core, *held((lead, resp, *chips, *steps)),
        us=20,
    )
    (field,) = call(
        whole_field,
        [(HBM, rhs.shape, f32)],
        core, *held((*parts, keep, swap(send))), *bu,
        scratch=[
            VMEM((WIDE, columns), f32),
            VMEM((elements, unknowns, columns), f32),
            dma((elements,)),
        ],
        us=1,
    )
    return by_row(field)


def solution(mesh):
    spec = P("sweep", "span", None, None)
    return jax.shard_map(
        per_device, mesh=mesh, in_specs=(spec,) * 6, out_specs=spec, check_vma=False
    )
```
